32 devices in a mesh: dp: 2 (over x), row: 4 (over y, core), col: 4 (over z).
Axes of the slice: x: 2, y: 2, z: 4, core: 2. Of those that a mesh axis runs over, the one named last changes fastest.
Arguments:
- grad_parts: float32 [2, 2, 4096, 5120], P('dp', None, 'row', 'col'), may hold values from -6 to 6
- weight: float32 [2, 4096, 5120], P(None, ('row', 'dp'), 'col'), may hold values from -6 to 6
- row_state: float32 [2, 4096], P(None, ('row', 'dp')), may hold values from 0.3 to 8, as said below
- col_state: float32 [2, 5120], P(None, 'col'), may hold values from 0.05 to 0.5
Outputs:
- new_weight: float32 [2, 4096, 5120], P(None, 'row', 'col')
- new_row_state: float32 [2, 4096], P(None, ('row', 'dp'))
- new_col_state: float32 [2, 5120], P(None, 'col')
The draws below stay inside these ranges and needn't reach their ends.
Inputs may be any that keep to these rules, and one draw needn't show every extreme that they name: `row_state`: positive row moments.
All inputs are finite; a program needn't handle non-finite values.
Results may differ from the reference program's by a relative error of at most 0.00002.
Values sent between devices are 32-bit elements; how exact they have to be, the bound alone decides.
A program may use at most 128 MiB of HBM per device.

```python
import math
import jax
import jax.numpy as jnp
from jax import lax

D = 4096
FF = 5120
EXPERTS = 2
N_DP = 2
N_ROW = 4


def draw_row_state(key, part):
    rows = jnp.arange(D)
    block = D // (N_ROW * N_DP)
    replica = rows // block % N_DP
    level = replica.astype(jnp.float32) / max(N_DP - 1, 1)
    base = 0.5 * 10.0 ** level
    jitter = jnp.exp(jax.random.uniform(key, (EXPERTS, D), jnp.float32, jnp.log(0.7), jnp.log(1.4)))
    return (base[None, :] * jitter).astype(jnp.float32)


def raised(array, stream_key, source, target, shards_of, factor):
    owner, partner = [(jnp.arange(array.shape[axis_at]) // (array.shape[axis_at] // shards_of)).reshape([-1 if axis == axis_at else 1 for axis in range(array.ndim)]) for axis_at in (source, target)]
    chosen = jax.random.permutation(stream_key, shards_of)[partner]
    strong = (owner == chosen) | (owner == (partner + shards_of // 2) % shards_of)
    return jnp.where(strong, factor * array, array)


def block_levels(stream_key, dims, split, least, largest):
    loudness = 1.0
    for dim, shards_of in split:
        steps = jax.random.uniform(jax.random.fold_in(jax.random.fold_in(stream_key, 6), dim), (shards_of,), jnp.float32, least / len(split), largest / len(split))
        loudness = loudness * jnp.repeat(jnp.exp(steps), dims[dim] // shards_of).reshape((-1,) + (1,) * (len(dims) - 1 - dim))
    return loudness


def gaussian(key, shape, deviation, bound, split=(), dtype=jnp.bfloat16):
    array = jax.random.normal(key, shape, jnp.float32) * deviation
    if len(split) > 0:
        array = block_levels(key, shape, split, -0.22, 0.18) * array
    return jnp.clip(array, min=-bound, max=bound).astype(dtype)


def gaussian_with(rng, dims, width, most, pieces, heavy, held_as=jnp.bfloat16):
    drawn = width * jax.random.normal(rng, dims, jnp.float32)
    if pieces:
        drawn = drawn * block_levels(rng, dims, pieces, -0.22, 0.18)
    return jnp.clip(raised(drawn, jax.random.fold_in(rng, 3), *heavy), -most, most).astype(held_as)


def setup_inputs(seed: int = 0) -> dict:
    seeds = jax.random.split(jax.random.key(seed), 5)
    grad_parts = gaussian_with(seeds[0], (N_DP, EXPERTS, D, FF), (1.0 / N_DP ** 0.5), 6.0, ((0, 2), (2, 4), (3, 4)), (0, 2, 2, 2.0), jnp.float32)
    weight = gaussian(seeds[1], (EXPERTS, D, FF), 1.0, 6.0, ((1, 8), (2, 4)), jnp.float32)
    row_state = draw_row_state(jax.random.fold_in(seeds[4], 71), 0)
    col_state = jnp.clip(jnp.exp(math.log(0.5) - 2.3025851 * jax.random.uniform(seeds[3], (EXPERTS, FF), jnp.float32) ** block_levels(seeds[3], (EXPERTS, FF), ((1, 4),), -0.2, 0.2)), 0.05, 0.5)
    return {"grad_parts": grad_parts, "weight": weight, "row_state": row_state, "col_state": col_state}


def reference(grad_parts, weight, row_state, col_state):
    decay = 1.0 - 2.0 ** (-0.8)
    grad = lax.optimization_barrier(jnp.sum(grad_parts, axis=0))
    sq = grad * grad + 1e-30
    new_row = decay * row_state + (1.0 - decay) * lax.optimization_barrier(jnp.sum(sq, axis=2)) / FF
    new_col = decay * col_state + (1.0 - decay) * lax.optimization_barrier(jnp.sum(sq, axis=1)) / D
    row_mean = lax.optimization_barrier(jnp.sum(new_row, axis=1)) / D
    vhat = new_row[:, :, None] * new_col[:, None, :] / row_mean[:, None, None]
    update = grad / jnp.sqrt(vhat)
    clip = jnp.maximum(1.0, jnp.sqrt(lax.optimization_barrier(jnp.sum(update * update, axis=(1, 2))) / (D * FF)))
    step_size = 0.3 * jnp.maximum(0.001, jnp.sqrt(lax.optimization_barrier(jnp.sum(weight * weight, axis=(1, 2))) / (D * FF)))
    new_weight = weight - (step_size / clip)[:, None, None] * update
    return (new_weight, new_row, new_col)
```

```python
import functools

import jax
import jax.numpy as jnp
from jax import lax
from jax.experimental import pallas as pl
from jax.experimental.pallas import tpu as pltpu
from jax.sharding import PartitionSpec as P

DECAY = 1.0 - 2.0 ** (-0.8)
MESH = pl.DeviceIdType.MESH
LANES = 128
CHUNK = 64
FLIGHT = 2


def adafactor(grad, weight, row_state, col_state, reduce_rows, reduce_cols, reduce_all, width, height):
    sq = grad * grad + 1e-30
    row_local = jnp.sum(sq, axis=2)
    weight_local = jnp.sum(weight * weight, axis=(1, 2))
    row_total, weight_part = reduce_rows(row_local, weight_local)
    new_row = DECAY * row_state + (1.0 - DECAY) * row_total / width
    col_local = jnp.sum(sq, axis=1)
    moment_local = jnp.sum(new_row, axis=1)
    col_total, moment_total, weight_total = reduce_cols(col_local, moment_local, weight_part)
    new_col = DECAY * col_state + (1.0 - DECAY) * col_total / height
    row_mean = moment_total / height
    vhat = new_row[:, :, None] * new_col[:, None, :] / row_mean[:, None, None]
    update = grad / jnp.sqrt(vhat)
    update_total = reduce_all(jnp.sum(update * update, axis=(1, 2)))
    clip = jnp.maximum(1.0, jnp.sqrt(update_total / (height * width)))
    step_size = 0.3 * jnp.maximum(0.001, jnp.sqrt(weight_total / (height * width)))
    new_weight = weight - (step_size / clip)[:, None, None] * update
    return (new_weight, new_row, new_col)


def plain_body(n_row, n_col, grad_parts, weight, row_state, col_state):
    grad = lax.psum_scatter(grad_parts[0], "dp", scatter_dimension=1, tiled=True)

    def reduce_rows(row_local, weight_local):
        return (lax.psum(row_local, "col"), weight_local)

    def reduce_cols(col_local, moment_local, weight_part):
        col_total, moment_total = lax.psum((col_local, moment_local), ("dp", "row"))
        weight_total = lax.psum(weight_part, ("dp", "row", "col"))
        return (col_total, moment_total, weight_total)

    def reduce_all(value):
        return lax.psum(value, ("dp", "row", "col"))

    width = grad_parts.shape[3] * n_col
    height = grad_parts.shape[2] * n_row
    new_shard, new_row, new_col = adafactor(
        grad, weight, row_state, col_state, reduce_rows, reduce_cols, reduce_all, width, height
    )
    new_weight = lax.all_gather(new_shard, "dp", axis=1, tiled=True)
    return (new_weight, new_row, new_col)


def kernel(
    n_row, n_col, gp, w, rs, cs, out, nrow, ncol,
    got, own, wv, part, colacc, colscale, alpha, rowbuf, colbuf, abuf, bbuf,
    load_sem, rs_send, rs_recv, ag_send, ag_recv,
    z_send, z_recv, g_send, g_recv,
):
    experts, half, cols = w.shape
    width, height = cols * n_col, 2 * half * n_row
    group = 2 * n_row
    blocks = half // LANES
    lane_blocks = cols // LANES
    per = half // CHUNK
    total = experts * per
    dp, row, col = lax.axis_index("dp"), lax.axis_index("row"), lax.axis_index("col")
    me = dp * n_row + row
    mine = pl.multiple_of(dp * half, CHUNK)
    theirs = pl.multiple_of((1 - dp) * half, CHUNK)
    partner = {"dp": 1 - dp}

    def col_peer(p):
        return {"col": lax.rem(col + p, n_col)}

    def group_peer(p):
        peer = lax.rem(me + p, group)
        return {"dp": lax.div(peer, n_row), "row": lax.rem(peer, n_row)}

    loads = []
    for e in range(experts):
        loads.append((
            pltpu.make_async_copy(gp.at[0, e, pl.ds(mine, half)], own.at[e], load_sem.at[2 * e]),
            pltpu.make_async_copy(w.at[e], wv.at[e], load_sem.at[2 * e + 1]),
        ))
    for pair in loads:
        for load in pair:
            load.start()

    barrier = pltpu.get_barrier_semaphore()
    for p in range(1, group):
        pl.semaphore_signal(barrier, inc=1, device_id=group_peer(p), device_id_type=MESH)
    for p in range(1, n_col):
        pl.semaphore_signal(barrier, inc=1, device_id=col_peer(p), device_id_type=MESH)
    pl.semaphore_wait(barrier, group + n_col - 2)

    def scatter(s):
        e, k = divmod(s, per)
        return pltpu.make_async_remote_copy(
            src_ref=gp.at[0, e, pl.ds(pl.multiple_of(theirs + k * CHUNK, CHUNK), CHUNK)],
            dst_ref=got.at[e, pl.ds(k * CHUNK, CHUNK)],
            send_sem=rs_send.at[s % FLIGHT], recv_sem=rs_recv.at[s],
            device_id=partner, device_id_type=MESH,
        )

    def gather(a):
        e, k = divmod(a, per)
        rows = out.at[e, pl.ds(pl.multiple_of(mine + k * CHUNK, CHUNK), CHUNK)]
        return pltpu.make_async_remote_copy(
            src_ref=rows,
            dst_ref=rows,
            send_sem=ag_send.at[a % FLIGHT], recv_sem=ag_recv.at[a],
            device_id=partner, device_id_type=MESH,
        )

    def exchange(buf, e, slot, count, peer_of, send, recv, which):
        return [
            pltpu.make_async_remote_copy(
                src_ref=buf.at[e, slot], dst_ref=buf.at[e, slot],
                send_sem=send.at[e, which, p - 1], recv_sem=recv.at[e, which, p - 1],
                device_id=peer_of(p), device_id_type=MESH,
            )
            for p in range(1, count)
        ]

    def row_exchange(e):
        return exchange(rowbuf, e, col, n_col, col_peer, z_send, z_recv, 0)

    def col_exchange(e):
        return exchange(colbuf, e, me, group, group_peer, g_send, g_recv, 0)

    def a_exchange(e):
        return exchange(abuf, e, col, n_col, col_peer, z_send, z_recv, 1)

    def b_exchange(e):
        return exchange(bbuf, e, me, group, group_peer, g_send, g_recv, 1)

    def start_all(copies):
        for copy in copies:
            copy.start()

    def wait_all(copies):
        for copy in copies:
            copy.wait()

    def summed(buf, e, count):
        value = buf[e, 0]
        for i in range(1, count):
            value = value + buf[e, i]
        return value

    def add_chunk(s):
        e, k = divmod(s, per)

        def step(i, acc):
            rows = pl.ds(pl.multiple_of(k * CHUNK + i * 8, 8), 8)
            g = own[e, rows, :] + got[e, rows, :]
            own[e, rows, :] = g
            sq = g * g + 1e-30
            lanes = sq[:, :LANES]
            for j in range(1, lane_blocks):
                lanes = lanes + sq[:, j * LANES:(j + 1) * LANES]
            part[e, rows, :] = lanes
            return acc + sq

        first = jnp.zeros((8, cols), jnp.float32) if k == 0 else colacc[e]
        colacc[e] = lax.fori_loop(0, CHUNK // 8, step, first)

    def moments_out(e):
        colbuf[e, me] = jnp.sum(colacc[e], axis=0, keepdims=True)
        for b in range(blocks):
            block = part[e, b * LANES:(b + 1) * LANES, :]
            rowbuf[e, col, b:b + 1, :] = jnp.sum(block.T, axis=0, keepdims=True)
        start_all(row_exchange(e))
        start_all(col_exchange(e))

    def moments_in(e):
        wait_all(row_exchange(e))
        row_total = summed(rowbuf, e, n_col)
        moment = jnp.zeros((1, LANES), jnp.float32)
        for b in range(blocks):
            at = slice(b * LANES, (b + 1) * LANES)
            new_row = DECAY * rs[e:e + 1, at] + (1.0 - DECAY) * row_total[b:b + 1, :] / width
            nrow[e:e + 1, at] = new_row
            moment = moment + new_row
            part[e, at, :] = jnp.broadcast_to(lax.rsqrt(new_row), (LANES, LANES)).T
        wait_all(col_exchange(e))
        new_col = DECAY * cs[e:e + 1, :] + (1.0 - DECAY) * summed(colbuf, e, group) / height
        ncol[e:e + 1, :] = new_col
        colscale[e] = jnp.broadcast_to(lax.rsqrt(new_col), (8, cols))
        bbuf[e, me, 16:24, :] = jnp.broadcast_to(moment * 0.125, (8, LANES))

    def normalise(e):
        loads[e][1].wait()

        def step(i, sums):
            upd, wgt = sums
            rows = pl.ds(pl.multiple_of(i * 8, 8), 8)
            scale = part[e, rows, :]
            for j in range(lane_blocks):
                at = slice(j * LANES, (j + 1) * LANES)
                t = own[e, rows, at] * (scale * colscale[e, :, at])
                own[e, rows, at] = t
                upd = upd + t * t
                v = wv[e, rows, at]
                wgt = wgt + v * v
            return upd, wgt

        zero = jnp.zeros((8, LANES), jnp.float32)
        upd, wgt = lax.fori_loop(0, half // 8, step, (zero, zero))
        abuf[e, col, 0:8, :] = upd
        abuf[e, col, 8:16, :] = wgt
        start_all(a_exchange(e))

    def tile_sums_in(e):
        wait_all(a_exchange(e))
        bbuf[e, me, 0:16, :] = summed(abuf, e, n_col)
        start_all(b_exchange(e))

    def scale_in(e):
        wait_all(b_exchange(e))
        sums = summed(bbuf, e, group)

        def whole(at):
            return jnp.sum(jnp.sum(sums[at:at + 8, :], axis=0, keepdims=True), axis=1, keepdims=True)

        size = float(width * height)
        row_mean = whole(16) / height
        clip = jnp.maximum(1.0, jnp.sqrt(row_mean * whole(0) / size))
        step_size = 0.3 * jnp.maximum(0.001, jnp.sqrt(whole(8) / size))
        alpha[e] = jnp.broadcast_to(step_size / clip * jnp.sqrt(row_mean), (8, LANES))

    def apply(e):
        def step(i, carry):
            rows = pl.ds(pl.multiple_of(i * 8, 8), 8)
            dest = pl.ds(pl.multiple_of(mine + i * 8, 8), 8)
            a = alpha[e]
            for j in range(lane_blocks):
                at = slice(j * LANES, (j + 1) * LANES)
                out[e, dest, at] = wv[e, rows, at] - a * own[e, rows, at]
            return carry

        lax.fori_loop(0, half // 8, step, 0)

    def next_send(n):
        if n >= 2 * total:
            return
        if n >= FLIGHT:
            before = n - FLIGHT
            if before < total:
                scatter(before).wait_send()
            else:
                gather(before - total).wait_send()
        if n < total:
            scatter(n).start()
        else:
            gather(n - total).start()

    for n in range(FLIGHT):
        next_send(n)
    after = {
        per - 1: [moments_out],
        per + 1: [moments_in, normalise],
        per + 2: [tile_sums_in],
        per + 3: [scale_in, apply],
    }
    for n in range(2 * total):
        e, k = divmod(n, per)
        if n < total:
            if k == 0:
                loads[e][0].wait()
            scatter(n).wait_recv()
            next_send(n + FLIGHT)
            add_chunk(n)
        else:
            next_send(n + FLIGHT)
        for done in range(experts):
            for task in after.get(n - done * per, []):
                task(done)
    for n in range(2 * total - FLIGHT, 2 * total):
        gather(n - total).wait_send()
    for a in range(total):
        gather(a).wait_recv()


def fused_body(n_row, n_col, grad_parts, weight, row_state, col_state):
    experts, half, cols = weight.shape
    group = 2 * n_row
    blocks = half // LANES
    total = experts * (half // CHUNK)
    f32 = jnp.float32
    hbm = pl.BlockSpec(memory_space=pltpu.HBM)
    vmem = pl.BlockSpec(memory_space=pltpu.VMEM)
    dma = pltpu.SemaphoreType.DMA
    return pl.pallas_call(
        functools.partial(kernel, n_row, n_col),
        out_shape=(
            jax.ShapeDtypeStruct((experts, 2 * half, cols), f32),
            jax.ShapeDtypeStruct(row_state.shape, f32),
            jax.ShapeDtypeStruct(col_state.shape, f32),
        ),
        in_specs=[hbm, hbm, vmem, vmem],
        out_specs=(vmem, vmem, vmem),
        scratch_shapes=[
            pltpu.VMEM((experts, half, cols), f32),
            pltpu.VMEM((experts, half, cols), f32),
            pltpu.VMEM((experts, half, cols), f32),
            pltpu.VMEM((experts, half, LANES), f32),
            pltpu.VMEM((experts, 8, cols), f32),
            pltpu.VMEM((experts, 8, cols), f32),
            pltpu.VMEM((experts, 8, LANES), f32),
            pltpu.VMEM((experts, n_col, blocks, LANES), f32),
            pltpu.VMEM((experts, group, 1, cols), f32),
            pltpu.VMEM((experts, n_col, 16, LANES), f32),
            pltpu.VMEM((experts, group, 24, LANES), f32),
            dma((2 * experts,)),
            dma((FLIGHT,)),
            dma((total,)),
            dma((FLIGHT,)),
            dma((total,)),
            dma((experts, 2, n_col - 1)),
            dma((experts, 2, n_col - 1)),
            dma((experts, 2, group - 1)),
            dma((experts, 2, group - 1)),
        ],
        compiler_params=pltpu.CompilerParams(
            collective_id=0, has_side_effects=True, vmem_limit_bytes=50 * 1024 * 1024
        ),
        cost_estimate=pl.CostEstimate(
            flops=20 * weight.size, bytes_accessed=20 * weight.size, transcendentals=0
        ),
        name="fused_step",
    )(grad_parts, weight, row_state, col_state)


def solution(mesh):
    placed = (
        P("dp", None, "row", "col"),
        P(None, ("row", "dp"), "col"),
        P(None, ("row", "dp")),
        P(None, "col"),
    )
    body = fused_body if mesh.shape["dp"] == 2 else plain_body
    return jax.shard_map(
        functools.partial(body, mesh.shape["row"], mesh.shape["col"]),
        mesh=mesh,
        in_specs=placed,
        out_specs=(P(None, "row", "col"), P(None, ("row", "dp")), P(None, "col")),
        check_vma=False,
    )
```

```python
import functools

import jax
import jax.numpy as jnp
from jax import lax
from jax.experimental import pallas as pl
from jax.experimental.pallas import tpu as pltpu
from jax.sharding import PartitionSpec as P

DECAY = 1.0 - 2.0 ** (-0.8)
MESH = pl.DeviceIdType.MESH
LANES = 128
CHUNK = 32
FLIGHT = 4
PIECE = 512


def adafactor(grad, weight, row_state, col_state, reduce_rows, reduce_cols, reduce_all, width, height):
    sq = grad * grad + 1e-30
    row_local = jnp.sum(sq, axis=2)
    weight_local = jnp.sum(weight * weight, axis=(1, 2))
    row_total, weight_part = reduce_rows(row_local, weight_local)
    new_row = DECAY * row_state + (1.0 - DECAY) * row_total / width
    col_local = jnp.sum(sq, axis=1)
    moment_local = jnp.sum(new_row, axis=1)
    col_total, moment_total, weight_total = reduce_cols(col_local, moment_local, weight_part)
    new_col = DECAY * col_state + (1.0 - DECAY) * col_total / height
    row_mean = moment_total / height
    vhat = new_row[:, :, None] * new_col[:, None, :] / row_mean[:, None, None]
    update = grad / jnp.sqrt(vhat)
    update_total = reduce_all(jnp.sum(update * update, axis=(1, 2)))
    clip = jnp.maximum(1.0, jnp.sqrt(update_total / (height * width)))
    step_size = 0.3 * jnp.maximum(0.001, jnp.sqrt(weight_total / (height * width)))
    new_weight = weight - (step_size / clip)[:, None, None] * update
    return (new_weight, new_row, new_col)


def plain_body(n_row, n_col, grad_parts, weight, row_state, col_state):
    grad = lax.psum_scatter(grad_parts[0], "dp", scatter_dimension=1, tiled=True)

    def reduce_rows(row_local, weight_local):
        return (lax.psum(row_local, "col"), weight_local)

    def reduce_cols(col_local, moment_local, weight_part):
        col_total, moment_total = lax.psum((col_local, moment_local), ("dp", "row"))
        weight_total = lax.psum(weight_part, ("dp", "row", "col"))
        return (col_total, moment_total, weight_total)

    def reduce_all(value):
        return lax.psum(value, ("dp", "row", "col"))

    width = grad_parts.shape[3] * n_col
    height = grad_parts.shape[2] * n_row
    new_shard, new_row, new_col = adafactor(
        grad, weight, row_state, col_state, reduce_rows, reduce_cols, reduce_all, width, height
    )
    new_weight = lax.all_gather(new_shard, "dp", axis=1, tiled=True)
    return (new_weight, new_row, new_col)


def kernel(
    n_row, n_col, gp, w, rs_in, cs_in, out, nrow, ncol,
    rs, cs, got, own, wv, part, colacc, colscale, alpha, rowbuf, colbuf, abuf, bbuf,
    load_sem, rs_send, rs_recv, ag_send, ag_recv,
    z_send, z_recv, g_send, g_recv,
):
    experts, half, cols = w.shape
    width, height = cols * n_col, 2 * half * n_row
    group = 2 * n_row
    blocks = half // LANES
    lane_blocks = cols // LANES
    per = half // CHUNK
    total = experts * per
    dp, row, col = lax.axis_index("dp"), lax.axis_index("row"), lax.axis_index("col")
    me = dp * n_row + row
    mine = pl.multiple_of(dp * half, CHUNK)
    theirs = pl.multiple_of((1 - dp) * half, CHUNK)
    partner = {"dp": 1 - dp}

    def col_peer(p):
        return {"col": lax.rem(col + p, n_col)}

    def group_peer(p):
        peer = lax.rem(me + p, group)
        return {"dp": lax.div(peer, n_row), "row": lax.rem(peer, n_row)}

    loads = []
    for e in range(experts):
        loads.append((
            pltpu.make_async_copy(gp.at[0, e, pl.ds(mine, half)], own.at[e], load_sem.at[2 * e]),
            pltpu.make_async_copy(w.at[e], wv.at[e], load_sem.at[2 * e + 1]),
        ))
    states = (
        pltpu.make_async_copy(rs_in, rs, load_sem.at[2 * experts]),
        pltpu.make_async_copy(cs_in, cs, load_sem.at[2 * experts + 1]),
    )
    for load in [load for pair in loads for load in pair] + list(states):
        load.start()

    barrier = pltpu.get_barrier_semaphore()
    for p in range(1, group):
        pl.semaphore_signal(barrier, inc=1, device_id=group_peer(p), device_id_type=MESH)
    for p in range(1, n_col):
        pl.semaphore_signal(barrier, inc=1, device_id=col_peer(p), device_id_type=MESH)
    pl.semaphore_wait(barrier, group + n_col - 2)

    def scatter(s):
        e, k = divmod(s, per)
        return pltpu.make_async_remote_copy(
            src_ref=gp.at[0, e, pl.ds(pl.multiple_of(theirs + k * CHUNK, CHUNK), CHUNK)],
            dst_ref=got.at[e, pl.ds(k * CHUNK, CHUNK)],
            send_sem=rs_send.at[s % FLIGHT], recv_sem=rs_recv.at[s],
            device_id=partner, device_id_type=MESH,
        )

    def gather(a):
        e, k = divmod(a, per)
        rows = out.at[e, pl.ds(pl.multiple_of(mine + k * CHUNK, CHUNK), CHUNK)]
        return pltpu.make_async_remote_copy(
            src_ref=rows,
            dst_ref=rows,
            send_sem=ag_send.at[a % FLIGHT], recv_sem=ag_recv.at[a],
            device_id=partner, device_id_type=MESH,
        )

    def exchange(buf, e, slot, count, peer_of, send, recv, which):
        return [
            pltpu.make_async_remote_copy(
                src_ref=buf.at[e, slot], dst_ref=buf.at[e, slot],
                send_sem=send.at[e, which, p - 1], recv_sem=recv.at[e, which, p - 1],
                device_id=peer_of(p), device_id_type=MESH,
            )
            for p in range(1, count)
        ]

    def row_exchange(e):
        return exchange(rowbuf, e, col, n_col, col_peer, z_send, z_recv, 0)

    def col_exchange(e):
        return exchange(colbuf, e, me, group, group_peer, g_send, g_recv, 0)

    def a_exchange(e):
        return exchange(abuf, e, col, n_col, col_peer, z_send, z_recv, 1)

    def b_exchange(e):
        return exchange(bbuf, e, me, group, group_peer, g_send, g_recv, 1)

    def start_all(copies):
        for copy in copies:
            copy.start()

    def wait_all(copies):
        for copy in copies:
            copy.wait()

    def summed(buf, e, count):
        value = buf[e, 0]
        for i in range(1, count):
            value = value + buf[e, i]
        return value

    def add_chunk(s):
        e, k = divmod(s, per)

        def step(i, acc):
            rows = pl.ds(pl.multiple_of(k * CHUNK + i * 8, 8), 8)
            g = own[e, rows, :] + got[e, rows, :]
            own[e, rows, :] = g
            sq = g * g + 1e-30
            lanes = sq[:, :LANES]
            for j in range(1, lane_blocks):
                lanes = lanes + sq[:, j * LANES:(j + 1) * LANES]
            part[e, rows, :] = lanes
            return acc + sq

        first = jnp.zeros((8, cols), jnp.float32) if k == 0 else colacc[e]
        colacc[e] = lax.fori_loop(0, CHUNK // 8, step, first)

    def moments_out(e):
        colbuf[e, me] = jnp.sum(colacc[e], axis=0, keepdims=True)
        for b in range(blocks):
            block = part[e, b * LANES:(b + 1) * LANES, :]
            rowbuf[e, col, b:b + 1, :] = jnp.sum(block.T, axis=0, keepdims=True)
        start_all(row_exchange(e))
        start_all(col_exchange(e))

    def moments_in(e):
        if e == 0:
            for load in states:
                load.wait()
        wait_all(row_exchange(e))
        row_total = summed(rowbuf, e, n_col)
        moment = jnp.zeros((1, LANES), jnp.float32)
        for b in range(blocks):
            at = slice(b * LANES, (b + 1) * LANES)
            new_row = DECAY * rs[e:e + 1, at] + (1.0 - DECAY) * row_total[b:b + 1, :] / width
            nrow[e:e + 1, at] = new_row
            moment = moment + new_row
            part[e, at, :] = jnp.broadcast_to(lax.rsqrt(new_row), (LANES, LANES)).T
        wait_all(col_exchange(e))
        new_col = DECAY * cs[e:e + 1, :] + (1.0 - DECAY) * summed(colbuf, e, group) / height
        ncol[e:e + 1, :] = new_col
        colscale[e] = jnp.broadcast_to(lax.rsqrt(new_col), (8, cols))
        bbuf[e, me, 16:24, :] = jnp.broadcast_to(moment * 0.125, (8, LANES))

    def normalise(e):
        loads[e][1].wait()

        def step(i, sums):
            upd, wgt = sums
            rows = pl.ds(pl.multiple_of(i * 8, 8), 8)
            scale = part[e, rows, :]
            for j in range(lane_blocks):
                at = slice(j * LANES, (j + 1) * LANES)
                t = own[e, rows, at] * (scale * colscale[e, :, at])
                own[e, rows, at] = t
                upd = upd + t * t
                v = wv[e, rows, at]
                wgt = wgt + v * v
            return upd, wgt

        zero = jnp.zeros((8, LANES), jnp.float32)
        upd, wgt = lax.fori_loop(0, half // 8, step, (zero, zero))
        abuf[e, col, 0:8, :] = upd
        abuf[e, col, 8:16, :] = wgt
        start_all(a_exchange(e))

    def tile_sums_in(e):
        wait_all(a_exchange(e))
        bbuf[e, me, 0:16, :] = summed(abuf, e, n_col)
        start_all(b_exchange(e))

    def scale_in(e):
        wait_all(b_exchange(e))
        sums = summed(bbuf, e, group)

        def whole(at):
            return jnp.sum(jnp.sum(sums[at:at + 8, :], axis=0, keepdims=True), axis=1, keepdims=True)

        size = float(width * height)
        row_mean = whole(16) / height
        clip = jnp.maximum(1.0, jnp.sqrt(row_mean * whole(0) / size))
        step_size = 0.3 * jnp.maximum(0.001, jnp.sqrt(whole(8) / size))
        alpha[e] = jnp.broadcast_to(step_size / clip * jnp.sqrt(row_mean), (8, LANES))

    def apply(e):
        def step(i, carry):
            rows = pl.ds(pl.multiple_of(i * 8, 8), 8)
            dest = pl.ds(pl.multiple_of(mine + i * 8, 8), 8)
            a = alpha[e]
            for j in range(lane_blocks):
                at = slice(j * LANES, (j + 1) * LANES)
                out[e, dest, at] = wv[e, rows, at] - a * own[e, rows, at]
            return carry

        lax.fori_loop(0, half // 8, step, 0)

    def next_send(n):
        if n >= 2 * total:
            return
        if n >= FLIGHT:
            before = n - FLIGHT
            if before < total:
                scatter(before).wait_send()
            else:
                gather(before - total).wait_send()
        if n < total:
            scatter(n).start()
        else:
            gather(n - total).start()

    for n in range(FLIGHT):
        next_send(n)
    after = {
        per - 1: [moments_out],
        per + 5: [moments_in, normalise],
        per + 7: [tile_sums_in],
        per + 11: [scale_in, apply],
    }
    for n in range(2 * total):
        e, k = divmod(n, per)
        if n < total:
            if k == 0:
                loads[e][0].wait()
            scatter(n).wait_recv()
            next_send(n + FLIGHT)
            add_chunk(n)
        else:
            next_send(n + FLIGHT)
        for done in range(experts):
            for task in after.get(n - done * per, []):
                task(done)
    for n in range(2 * total - FLIGHT, 2 * total):
        gather(n - total).wait_send()
    for a in range(total):
        gather(a).wait_recv()


def write_out(sources, targets, sems):
    copies = []
    for source, target in zip(sources, targets):
        if source.ndim == 3:
            step = min(PIECE, source.shape[1])
            for e in range(source.shape[0]):
                for r in range(0, source.shape[1], step):
                    copies.append((source.at[e, pl.ds(r, step)], target.at[e, pl.ds(r, step)]))
        else:
            copies.append((source, target))
    copies = [pltpu.make_async_copy(a, b, sems.at[i]) for i, (a, b) in enumerate(copies)]
    for copy in copies:
        copy.start()
    for copy in copies:
        copy.wait()


def writer(a, b, c, x, y, z, sems):
    write_out((a, b, c), (x, y, z), sems)


def written(results):
    anywhere = pl.BlockSpec(memory_space=pl.ANY)
    hbm = pl.BlockSpec(memory_space=pltpu.HBM)
    big = results[0].shape
    count = big[0] * (big[1] // min(PIECE, big[1])) + 2
    return pl.pallas_call(
        writer,
        out_shape=tuple(jax.ShapeDtypeStruct(r.shape, r.dtype) for r in results),
        in_specs=[anywhere] * 3,
        out_specs=(hbm,) * 3,
        scratch_shapes=[pltpu.SemaphoreType.DMA((count,))],
        compiler_params=pltpu.CompilerParams(vmem_limit_bytes=1024 * 1024),
        name="write_out",
    )(*results)


def fused_body(n_row, n_col, grad_parts, weight, row_state, col_state):
    experts, half, cols = weight.shape
    group = 2 * n_row
    blocks = half // LANES
    total = experts * (half // CHUNK)
    f32 = jnp.float32
    hbm = pl.BlockSpec(memory_space=pltpu.HBM)
    vmem = pl.BlockSpec(memory_space=pltpu.VMEM)
    dma = pltpu.SemaphoreType.DMA
    results = pl.pallas_call(
        functools.partial(kernel, n_row, n_col),
        out_shape=(
            pltpu.VMEM((experts, 2 * half, cols), f32),
            pltpu.VMEM(row_state.shape, f32),
            pltpu.VMEM(col_state.shape, f32),
        ),
        in_specs=[hbm] * 4,
        out_specs=(vmem, vmem, vmem),
        scratch_shapes=[
            pltpu.VMEM(row_state.shape, f32),
            pltpu.VMEM(col_state.shape, f32),
            pltpu.VMEM((experts, half, cols), f32),
            pltpu.VMEM((experts, half, cols), f32),
            pltpu.VMEM((experts, half, cols), f32),
            pltpu.VMEM((experts, half, LANES), f32),
            pltpu.VMEM((experts, 8, cols), f32),
            pltpu.VMEM((experts, 8, cols), f32),
            pltpu.VMEM((experts, 8, LANES), f32),
            pltpu.VMEM((experts, n_col, blocks, LANES), f32),
            pltpu.VMEM((experts, group, 1, cols), f32),
            pltpu.VMEM((experts, n_col, 16, LANES), f32),
            pltpu.VMEM((experts, group, 24, LANES), f32),
            dma((2 * experts + 2,)),
            dma((FLIGHT,)),
            dma((total,)),
            dma((FLIGHT,)),
            dma((total,)),
            dma((experts, 2, n_col - 1)),
            dma((experts, 2, n_col - 1)),
            dma((experts, 2, group - 1)),
            dma((experts, 2, group - 1)),
        ],
        compiler_params=pltpu.CompilerParams(
            collective_id=0, has_side_effects=True, vmem_limit_bytes=30 * 1024 * 1024
        ),
        cost_estimate=pl.CostEstimate(
            flops=20 * weight.size, bytes_accessed=20 * weight.size, transcendentals=0
        ),
        name="fused_step",
    )(*[
        pltpu.with_memory_space_constraint(x, pltpu.HBM)
        for x in (grad_parts, weight, row_state, col_state)
    ])
    return written(results)


def solution(mesh):
    placed = (
        P("dp", None, "row", "col"),
        P(None, ("row", "dp"), "col"),
        P(None, ("row", "dp")),
        P(None, "col"),
    )
    body = fused_body if mesh.shape["dp"] == 2 else plain_body
    return jax.shard_map(
        functools.partial(body, mesh.shape["row"], mesh.shape["col"]),
        mesh=mesh,
        in_specs=placed,
        out_specs=(P(None, "row", "col"), P(None, ("row", "dp")), P(None, "col")),
        check_vma=False,
    )
```

```python
import functools

import jax
import jax.numpy as jnp
from jax import lax
from jax.experimental import pallas as pl
from jax.experimental.pallas import tpu as pltpu
from jax.sharding import PartitionSpec as P

DECAY = 1.0 - 2.0 ** (-0.8)
MESH = pl.DeviceIdType.MESH
LANES = 128
CHUNK = 32
FLIGHT = 6
PIECE = 128


def adafactor(grad, weight, row_state, col_state, reduce_rows, reduce_cols, reduce_all, width, height):
    sq = grad * grad + 1e-30
    row_local = jnp.sum(sq, axis=2)
    weight_local = jnp.sum(weight * weight, axis=(1, 2))
    row_total, weight_part = reduce_rows(row_local, weight_local)
    new_row = DECAY * row_state + (1.0 - DECAY) * row_total / width
    col_local = jnp.sum(sq, axis=1)
    moment_local = jnp.sum(new_row, axis=1)
    col_total, moment_total, weight_total = reduce_cols(col_local, moment_local, weight_part)
    new_col = DECAY * col_state + (1.0 - DECAY) * col_total / height
    row_mean = moment_total / height
    vhat = new_row[:, :, None] * new_col[:, None, :] / row_mean[:, None, None]
    update = grad / jnp.sqrt(vhat)
    update_total = reduce_all(jnp.sum(update * update, axis=(1, 2)))
    clip = jnp.maximum(1.0, jnp.sqrt(update_total / (height * width)))
    step_size = 0.3 * jnp.maximum(0.001, jnp.sqrt(weight_total / (height * width)))
    new_weight = weight - (step_size / clip)[:, None, None] * update
    return (new_weight, new_row, new_col)


def plain_body(n_row, n_col, grad_parts, weight, row_state, col_state):
    grad = lax.psum_scatter(grad_parts[0], "dp", scatter_dimension=1, tiled=True)

    def reduce_rows(row_local, weight_local):
        return (lax.psum(row_local, "col"), weight_local)

    def reduce_cols(col_local, moment_local, weight_part):
        col_total, moment_total = lax.psum((col_local, moment_local), ("dp", "row"))
        weight_total = lax.psum(weight_part, ("dp", "row", "col"))
        return (col_total, moment_total, weight_total)

    def reduce_all(value):
        return lax.psum(value, ("dp", "row", "col"))

    width = grad_parts.shape[3] * n_col
    height = grad_parts.shape[2] * n_row
    new_shard, new_row, new_col = adafactor(
        grad, weight, row_state, col_state, reduce_rows, reduce_cols, reduce_all, width, height
    )
    new_weight = lax.all_gather(new_shard, "dp", axis=1, tiled=True)
    return (new_weight, new_row, new_col)


def kernel(
    n_row, n_col, gp, w, rs_in, cs_in, out, nrow, ncol,
    rs, cs, got, own, wv, part, colacc, colscale, alpha, rowbuf, colbuf, abuf, bbuf,
    load_sem, rs_send, rs_recv, ag_send, ag_recv,
    z_send, z_recv, g_send, g_recv,
):
    experts, half, cols = w.shape
    width, height = cols * n_col, 2 * half * n_row
    group = 2 * n_row
    blocks = half // LANES
    lane_blocks = cols // LANES
    per = half // CHUNK
    total = experts * per
    dp, row, col = lax.axis_index("dp"), lax.axis_index("row"), lax.axis_index("col")
    me = dp * n_row + row
    mine = pl.multiple_of(dp * half, CHUNK)
    theirs = pl.multiple_of((1 - dp) * half, CHUNK)
    partner = {"dp": 1 - dp}

    def col_peer(p):
        return {"col": lax.rem(col + p, n_col)}

    def group_peer(p):
        peer = lax.rem(me + p, group)
        return {"dp": lax.div(peer, n_row), "row": lax.rem(peer, n_row)}

    loads = []
    for e in range(experts):
        loads.append((
            pltpu.make_async_copy(gp.at[0, e, pl.ds(mine, half)], own.at[e], load_sem.at[2 * e]),
            pltpu.make_async_copy(w.at[e], wv.at[e], load_sem.at[2 * e + 1]),
        ))
    states = (
        pltpu.make_async_copy(rs_in, rs, load_sem.at[2 * experts]),
        pltpu.make_async_copy(cs_in, cs, load_sem.at[2 * experts + 1]),
    )
    loads[0][0].start()

    barrier = pltpu.get_barrier_semaphore()
    for p in range(1, group):
        pl.semaphore_signal(barrier, inc=1, device_id=group_peer(p), device_id_type=MESH)
    for p in range(1, n_col):
        pl.semaphore_signal(barrier, inc=1, device_id=col_peer(p), device_id_type=MESH)
    pl.semaphore_wait(barrier, group + n_col - 2)

    def scatter(s):
        e, k = divmod(s, per)
        return pltpu.make_async_remote_copy(
            src_ref=gp.at[0, e, pl.ds(pl.multiple_of(theirs + k * CHUNK, CHUNK), CHUNK)],
            dst_ref=got.at[e, pl.ds(k * CHUNK, CHUNK)],
            send_sem=rs_send.at[s % FLIGHT], recv_sem=rs_recv.at[s],
            device_id=partner, device_id_type=MESH,
        )

    def gather(a):
        e, k = divmod(a, per)
        rows = out.at[e, pl.ds(pl.multiple_of(mine + k * CHUNK, CHUNK), CHUNK)]
        return pltpu.make_async_remote_copy(
            src_ref=rows,
            dst_ref=rows,
            send_sem=ag_send.at[a % FLIGHT], recv_sem=ag_recv.at[a],
            device_id=partner, device_id_type=MESH,
        )

    def exchange(buf, e, slot, count, peer_of, send, recv, which):
        return [
            pltpu.make_async_remote_copy(
                src_ref=buf.at[e, slot], dst_ref=buf.at[e, slot],
                send_sem=send.at[e, which, p - 1], recv_sem=recv.at[e, which, p - 1],
                device_id=peer_of(p), device_id_type=MESH,
            )
            for p in range(1, count)
        ]

    def row_exchange(e):
        return exchange(rowbuf, e, col, n_col, col_peer, z_send, z_recv, 0)

    def col_exchange(e):
        return exchange(colbuf, e, me, group, group_peer, g_send, g_recv, 0)

    def a_exchange(e):
        return exchange(abuf, e, col, n_col, col_peer, z_send, z_recv, 1)

    def b_exchange(e):
        return exchange(bbuf, e, me, group, group_peer, g_send, g_recv, 1)

    def start_all(copies):
        for copy in copies:
            copy.start()

    def wait_all(copies):
        for copy in copies:
            copy.wait()

    def summed(buf, e, count):
        value = buf[e, 0]
        for i in range(1, count):
            value = value + buf[e, i]
        return value

    def add_chunk(s):
        e, k = divmod(s, per)

        def step(i, acc):
            rows = pl.ds(pl.multiple_of(k * CHUNK + i * 8, 8), 8)
            g = own[e, rows, :] + got[e, rows, :]
            own[e, rows, :] = g
            sq = g * g + 1e-30
            lanes = sq[:, :LANES]
            for j in range(1, lane_blocks):
                lanes = lanes + sq[:, j * LANES:(j + 1) * LANES]
            part[e, rows, :] = lanes
            return acc + sq

        first = jnp.zeros((8, cols), jnp.float32) if k == 0 else colacc[e]
        colacc[e] = lax.fori_loop(0, CHUNK // 8, step, first)

    def moments_out(e):
        colbuf[e, me] = jnp.sum(colacc[e], axis=0, keepdims=True)
        for b in range(blocks):
            block = part[e, b * LANES:(b + 1) * LANES, :]
            rowbuf[e, col, b:b + 1, :] = jnp.sum(block.T, axis=0, keepdims=True)
        start_all(row_exchange(e))
        start_all(col_exchange(e))

    def moments_in(e):
        if e == 0:
            for load in states:
                load.wait()
        wait_all(row_exchange(e))
        row_total = summed(rowbuf, e, n_col)
        moment = jnp.zeros((1, LANES), jnp.float32)
        for b in range(blocks):
            at = slice(b * LANES, (b + 1) * LANES)
            new_row = DECAY * rs[e:e + 1, at] + (1.0 - DECAY) * row_total[b:b + 1, :] / width
            nrow[e:e + 1, at] = new_row
            moment = moment + new_row
            part[e, at, :] = jnp.broadcast_to(lax.rsqrt(new_row), (LANES, LANES)).T
        wait_all(col_exchange(e))
        new_col = DECAY * cs[e:e + 1, :] + (1.0 - DECAY) * summed(colbuf, e, group) / height
        ncol[e:e + 1, :] = new_col
        colscale[e] = jnp.broadcast_to(lax.rsqrt(new_col), (8, cols))
        bbuf[e, me, 16:24, :] = jnp.broadcast_to(moment * 0.125, (8, LANES))

    def normalise(e):
        loads[e][1].wait()

        def step(i, sums):
            upd, wgt = sums
            rows = pl.ds(pl.multiple_of(i * 8, 8), 8)
            scale = part[e, rows, :]
            for j in range(lane_blocks):
                at = slice(j * LANES, (j + 1) * LANES)
                t = own[e, rows, at] * (scale * colscale[e, :, at])
                own[e, rows, at] = t
                upd = upd + t * t
                v = wv[e, rows, at]
                wgt = wgt + v * v
            return upd, wgt

        zero = jnp.zeros((8, LANES), jnp.float32)
        upd, wgt = lax.fori_loop(0, half // 8, step, (zero, zero))
        abuf[e, col, 0:8, :] = upd
        abuf[e, col, 8:16, :] = wgt
        start_all(a_exchange(e))

    def tile_sums_in(e):
        wait_all(a_exchange(e))
        bbuf[e, me, 0:16, :] = summed(abuf, e, n_col)
        start_all(b_exchange(e))

    def scale_in(e):
        wait_all(b_exchange(e))
        sums = summed(bbuf, e, group)

        def whole(at):
            return jnp.sum(jnp.sum(sums[at:at + 8, :], axis=0, keepdims=True), axis=1, keepdims=True)

        size = float(width * height)
        row_mean = whole(16) / height
        clip = jnp.maximum(1.0, jnp.sqrt(row_mean * whole(0) / size))
        step_size = 0.3 * jnp.maximum(0.001, jnp.sqrt(whole(8) / size))
        alpha[e] = jnp.broadcast_to(step_size / clip * jnp.sqrt(row_mean), (8, LANES))

    def apply(e):
        def step(i, carry):
            rows = pl.ds(pl.multiple_of(i * 8, 8), 8)
            dest = pl.ds(pl.multiple_of(mine + i * 8, 8), 8)
            a = alpha[e]
            for j in range(lane_blocks):
                at = slice(j * LANES, (j + 1) * LANES)
                out[e, dest, at] = wv[e, rows, at] - a * own[e, rows, at]
            return carry

        lax.fori_loop(0, half // 8, step, 0)

    def next_send(n):
        if n >= 2 * total:
            return
        if n >= FLIGHT:
            before = n - FLIGHT
            if before < total:
                scatter(before).wait_send()
            else:
                gather(before - total).wait_send()
        if n < total:
            scatter(n).start()
        else:
            gather(n - total).start()

    for n in range(FLIGHT):
        next_send(n)
    for load in list(states) + [load for pair in loads for load in pair][1:]:
        load.start()
    after = {
        per - 1: [moments_out],
        per + 5: [moments_in, normalise],
        per + 6: [tile_sums_in],
        per + 9: [scale_in, apply],
    }
    for n in range(2 * total):
        e, k = divmod(n, per)
        if n < total:
            if k == 0:
                loads[e][0].wait()
            scatter(n).wait_recv()
            next_send(n + FLIGHT)
            add_chunk(n)
        else:
            next_send(n + FLIGHT)
        for done in range(experts):
            for task in after.get(n - done * per, []):
                task(done)
    for n in range(2 * total - FLIGHT, 2 * total):
        gather(n - total).wait_send()
    for a in range(total):
        gather(a).wait_recv()


def write_out(sources, targets, sems):
    copies = []
    for source, target in zip(sources, targets):
        if source.ndim == 3:
            step = min(PIECE, source.shape[1])
            for e in range(source.shape[0]):
                for r in range(0, source.shape[1], step):
                    copies.append((source.at[e, pl.ds(r, step)], target.at[e, pl.ds(r, step)]))
        else:
            copies.append((source, target))
    copies = [pltpu.make_async_copy(a, b, sems.at[i]) for i, (a, b) in enumerate(copies)]
    for copy in copies:
        copy.start()
    for copy in copies:
        copy.wait()


def writer(a, b, c, x, y, z, sems):
    write_out((a, b, c), (x, y, z), sems)


def written(results):
    anywhere = pl.BlockSpec(memory_space=pl.ANY)
    hbm = pl.BlockSpec(memory_space=pltpu.HBM)
    big = results[0].shape
    count = big[0] * (big[1] // min(PIECE, big[1])) + 2
    return pl.pallas_call(
        writer,
        out_shape=tuple(jax.ShapeDtypeStruct(r.shape, r.dtype) for r in results),
        in_specs=[anywhere] * 3,
        out_specs=(hbm,) * 3,
        scratch_shapes=[pltpu.SemaphoreType.DMA((count,))],
        compiler_params=pltpu.CompilerParams(vmem_limit_bytes=1024 * 1024),
        name="write_out",
    )(*results)


def fused_body(n_row, n_col, grad_parts, weight, row_state, col_state):
    experts, half, cols = weight.shape
    group = 2 * n_row
    blocks = half // LANES
    total = experts * (half // CHUNK)
    f32 = jnp.float32
    hbm = pl.BlockSpec(memory_space=pltpu.HBM)
    vmem = pl.BlockSpec(memory_space=pltpu.VMEM)
    dma = pltpu.SemaphoreType.DMA
    results = pl.pallas_call(
        functools.partial(kernel, n_row, n_col),
        out_shape=(
            pltpu.VMEM((experts, 2 * half, cols), f32),
            pltpu.VMEM(row_state.shape, f32),
            pltpu.VMEM(col_state.shape, f32),
        ),
        in_specs=[hbm] * 4,
        out_specs=(vmem, vmem, vmem),
        scratch_shapes=[
            pltpu.VMEM(row_state.shape, f32),
            pltpu.VMEM(col_state.shape, f32),
            pltpu.VMEM((experts, half, cols), f32),
            pltpu.VMEM((experts, half, cols), f32),
            pltpu.VMEM((experts, half, cols), f32),
            pltpu.VMEM((experts, half, LANES), f32),
            pltpu.VMEM((experts, 8, cols), f32),
            pltpu.VMEM((experts, 8, cols), f32),
            pltpu.VMEM((experts, 8, LANES), f32),
            pltpu.VMEM((experts, n_col, blocks, LANES), f32),
            pltpu.VMEM((experts, group, 1, cols), f32),
            pltpu.VMEM((experts, n_col, 16, LANES), f32),
            pltpu.VMEM((experts, group, 24, LANES), f32),
            dma((2 * experts + 2,)),
            dma((FLIGHT,)),
            dma((total,)),
            dma((FLIGHT,)),
            dma((total,)),
            dma((experts, 2, n_col - 1)),
            dma((experts, 2, n_col - 1)),
            dma((experts, 2, group - 1)),
            dma((experts, 2, group - 1)),
        ],
        compiler_params=pltpu.CompilerParams(
            collective_id=0, has_side_effects=True, vmem_limit_bytes=30 * 1024 * 1024
        ),
        cost_estimate=pl.CostEstimate(
            flops=20 * weight.size, bytes_accessed=20 * weight.size, transcendentals=0
        ),
        name="fused_step",
    )(*[
        pltpu.with_memory_space_constraint(x, pltpu.HBM)
        for x in (grad_parts, weight, row_state, col_state)
    ])
    return written(results)


def solution(mesh):
    placed = (
        P("dp", None, "row", "col"),
        P(None, ("row", "dp"), "col"),
        P(None, ("row", "dp")),
        P(None, "col"),
    )
    body = fused_body if mesh.shape["dp"] == 2 else plain_body
    return jax.shard_map(
        functools.partial(body, mesh.shape["row"], mesh.shape["col"]),
        mesh=mesh,
        in_specs=placed,
        out_specs=(P(None, "row", "col"), P(None, ("row", "dp")), P(None, "col")),
        check_vma=False,
    )
```

```python
import functools

import jax
import jax.numpy as jnp
from jax import lax
from jax.experimental import pallas as pl
from jax.experimental.pallas import tpu as pltpu
from jax.sharding import PartitionSpec as P

DECAY = 1.0 - 2.0 ** (-0.8)
MESH = pl.DeviceIdType.MESH
LANES = 128
CHUNK = 32
FLIGHT = 4
PIECE = 128


def adafactor(grad, weight, row_state, col_state, reduce_rows, reduce_cols, reduce_all, width, height):
    sq = grad * grad + 1e-30
    row_local = jnp.sum(sq, axis=2)
    weight_local = jnp.sum(weight * weight, axis=(1, 2))
    row_total, weight_part = reduce_rows(row_local, weight_local)
    new_row = DECAY * row_state + (1.0 - DECAY) * row_total / width
    col_local = jnp.sum(sq, axis=1)
    moment_local = jnp.sum(new_row, axis=1)
    col_total, moment_total, weight_total = reduce_cols(col_local, moment_local, weight_part)
    new_col = DECAY * col_state + (1.0 - DECAY) * col_total / height
    row_mean = moment_total / height
    vhat = new_row[:, :, None] * new_col[:, None, :] / row_mean[:, None, None]
    update = grad / jnp.sqrt(vhat)
    update_total = reduce_all(jnp.sum(update * update, axis=(1, 2)))
    clip = jnp.maximum(1.0, jnp.sqrt(update_total / (height * width)))
    step_size = 0.3 * jnp.maximum(0.001, jnp.sqrt(weight_total / (height * width)))
    new_weight = weight - (step_size / clip)[:, None, None] * update
    return (new_weight, new_row, new_col)


def plain_body(n_row, n_col, grad_parts, weight, row_state, col_state):
    grad = lax.psum_scatter(grad_parts[0], "dp", scatter_dimension=1, tiled=True)

    def reduce_rows(row_local, weight_local):
        return (lax.psum(row_local, "col"), weight_local)

    def reduce_cols(col_local, moment_local, weight_part):
        col_total, moment_total = lax.psum((col_local, moment_local), ("dp", "row"))
        weight_total = lax.psum(weight_part, ("dp", "row", "col"))
        return (col_total, moment_total, weight_total)

    def reduce_all(value):
        return lax.psum(value, ("dp", "row", "col"))

    width = grad_parts.shape[3] * n_col
    height = grad_parts.shape[2] * n_row
    new_shard, new_row, new_col = adafactor(
        grad, weight, row_state, col_state, reduce_rows, reduce_cols, reduce_all, width, height
    )
    new_weight = lax.all_gather(new_shard, "dp", axis=1, tiled=True)
    return (new_weight, new_row, new_col)


def kernel(
    n_row, n_col, gp, w, rs_in, cs_in, out, nrow, ncol,
    rs, cs, got, own, wv, part, colacc, colscale, alpha, rowbuf, colbuf, colpair, abuf, bbuf, bpair,
    load_sem, rs_send, rs_recv, ag_send, ag_recv,
    z_send, z_recv, y_send, y_recv, x_send, x_recv,
):
    experts, half, cols = w.shape
    width, height = cols * n_col, 2 * half * n_row
    blocks = half // LANES
    lane_blocks = cols // LANES
    per = half // CHUNK
    total = experts * per
    dp, row, col = lax.axis_index("dp"), lax.axis_index("row"), lax.axis_index("col")
    mine = pl.multiple_of(dp * half, CHUNK)
    theirs = pl.multiple_of((1 - dp) * half, CHUNK)
    partner = {"dp": 1 - dp}

    def col_peer(p):
        return {"col": lax.rem(col + p, n_col)}

    def row_peer(p):
        return {"row": lax.rem(row + p, n_row)}

    def dp_peer(p):
        return partner

    loads = []
    for e in range(experts):
        loads.append((
            pltpu.make_async_copy(gp.at[0, e, pl.ds(mine, half)], own.at[e], load_sem.at[2 * e]),
            pltpu.make_async_copy(w.at[e], wv.at[e], load_sem.at[2 * e + 1]),
        ))
    states = (
        pltpu.make_async_copy(rs_in, rs, load_sem.at[2 * experts]),
        pltpu.make_async_copy(cs_in, cs, load_sem.at[2 * experts + 1]),
    )
    loads[0][0].start()

    barrier = pltpu.get_barrier_semaphore()
    pl.semaphore_signal(barrier, inc=1, device_id=partner, device_id_type=MESH)
    for p in range(1, n_col):
        pl.semaphore_signal(barrier, inc=1, device_id=col_peer(p), device_id_type=MESH)
    for p in range(1, n_row):
        pl.semaphore_signal(barrier, inc=1, device_id=row_peer(p), device_id_type=MESH)
    pl.semaphore_wait(barrier, n_row + n_col - 1)

    def scatter(s):
        e, k = divmod(s, per)
        return pltpu.make_async_remote_copy(
            src_ref=gp.at[0, e, pl.ds(pl.multiple_of(theirs + k * CHUNK, CHUNK), CHUNK)],
            dst_ref=got.at[e, pl.ds(k * CHUNK, CHUNK)],
            send_sem=rs_send.at[s % FLIGHT], recv_sem=rs_recv.at[s],
            device_id=partner, device_id_type=MESH,
        )

    def gather(a):
        e, k = divmod(a, per)
        rows = out.at[e, pl.ds(pl.multiple_of(mine + k * CHUNK, CHUNK), CHUNK)]
        return pltpu.make_async_remote_copy(
            src_ref=rows,
            dst_ref=rows,
            send_sem=ag_send.at[a % FLIGHT], recv_sem=ag_recv.at[a],
            device_id=partner, device_id_type=MESH,
        )

    def exchange(buf, e, slot, count, peer_of, send, recv, which):
        return [
            pltpu.make_async_remote_copy(
                src_ref=buf.at[e, slot], dst_ref=buf.at[e, slot],
                send_sem=send.at[e, which, p - 1], recv_sem=recv.at[e, which, p - 1],
                device_id=peer_of(p), device_id_type=MESH,
            )
            for p in range(1, count)
        ]

    def row_exchange(e):
        return exchange(rowbuf, e, col, n_col, col_peer, z_send, z_recv, 0)

    def col_exchange(e):
        return exchange(colbuf, e, row, n_row, row_peer, y_send, y_recv, 0)

    def col_pair(e):
        return exchange(colpair, e, dp, 2, dp_peer, x_send, x_recv, 0)

    def a_exchange(e):
        return exchange(abuf, e, col, n_col, col_peer, z_send, z_recv, 1)

    def b_exchange(e):
        return exchange(bbuf, e, row, n_row, row_peer, y_send, y_recv, 1)

    def b_pair(e):
        return exchange(bpair, e, dp, 2, dp_peer, x_send, x_recv, 1)

    def start_all(copies):
        for copy in copies:
            copy.start()

    def wait_all(copies):
        for copy in copies:
            copy.wait()

    def summed(buf, e, count):
        value = buf[e, 0]
        for i in range(1, count):
            value = value + buf[e, i]
        return value

    def add_chunk(s):
        e, k = divmod(s, per)

        def step(i, acc):
            rows = pl.ds(pl.multiple_of(k * CHUNK + i * 8, 8), 8)
            g = own[e, rows, :] + got[e, rows, :]
            own[e, rows, :] = g
            sq = g * g + 1e-30
            lanes = sq[:, :LANES]
            for j in range(1, lane_blocks):
                lanes = lanes + sq[:, j * LANES:(j + 1) * LANES]
            part[e, rows, :] = lanes
            return acc + sq

        first = jnp.zeros((8, cols), jnp.float32) if k == 0 else colacc[e]
        colacc[e] = lax.fori_loop(0, CHUNK // 8, step, first)

    def moments_out(e):
        colbuf[e, row] = jnp.sum(colacc[e], axis=0, keepdims=True)
        for b in range(blocks):
            block = part[e, b * LANES:(b + 1) * LANES, :]
            rowbuf[e, col, b:b + 1, :] = jnp.sum(block.T, axis=0, keepdims=True)
        start_all(row_exchange(e))
        start_all(col_exchange(e))

    def columns_in(e):
        wait_all(col_exchange(e))
        colpair[e, dp] = summed(colbuf, e, n_row)
        start_all(col_pair(e))

    def moments_in(e):
        if e == 0:
            for load in states:
                load.wait()
        wait_all(row_exchange(e))
        row_total = summed(rowbuf, e, n_col)
        moment = jnp.zeros((1, LANES), jnp.float32)
        for b in range(blocks):
            at = slice(b * LANES, (b + 1) * LANES)
            new_row = DECAY * rs[e:e + 1, at] + (1.0 - DECAY) * row_total[b:b + 1, :] / width
            nrow[e:e + 1, at] = new_row
            moment = moment + new_row
            part[e, at, :] = jnp.broadcast_to(lax.rsqrt(new_row), (LANES, LANES)).T
        wait_all(col_pair(e))
        new_col = DECAY * cs[e:e + 1, :] + (1.0 - DECAY) * summed(colpair, e, 2) / height
        ncol[e:e + 1, :] = new_col
        colscale[e] = jnp.broadcast_to(lax.rsqrt(new_col), (8, cols))
        bbuf[e, row, 2:3, :] = moment

    def normalise(e):
        loads[e][1].wait()

        def step(i, sums):
            upd, wgt = sums
            rows = pl.ds(pl.multiple_of(i * 8, 8), 8)
            scale = part[e, rows, :]
            for j in range(lane_blocks):
                at = slice(j * LANES, (j + 1) * LANES)
                t = own[e, rows, at] * (scale * colscale[e, :, at])
                own[e, rows, at] = t
                upd = upd + t * t
                v = wv[e, rows, at]
                wgt = wgt + v * v
            return upd, wgt

        zero = jnp.zeros((8, LANES), jnp.float32)
        upd, wgt = lax.fori_loop(0, half // 8, step, (zero, zero))
        abuf[e, col, 0:1, :] = jnp.sum(upd, axis=0, keepdims=True)
        abuf[e, col, 1:2, :] = jnp.sum(wgt, axis=0, keepdims=True)
        start_all(a_exchange(e))

    def tile_sums_in(e):
        wait_all(a_exchange(e))
        bbuf[e, row, 0:2, :] = summed(abuf, e, n_col)
        start_all(b_exchange(e))

    def plane_sums_in(e):
        wait_all(b_exchange(e))
        bpair[e, dp] = summed(bbuf, e, n_row)
        start_all(b_pair(e))

    def scale_in(e):
        wait_all(b_pair(e))
        sums = jnp.sum(summed(bpair, e, 2), axis=1, keepdims=True)

        def whole(at):
            return sums[at:at + 1, :]

        size = float(width * height)
        row_mean = whole(2) / height
        clip = jnp.maximum(1.0, jnp.sqrt(row_mean * whole(0) / size))
        step_size = 0.3 * jnp.maximum(0.001, jnp.sqrt(whole(1) / size))
        alpha[e] = jnp.broadcast_to(step_size / clip * jnp.sqrt(row_mean), (8, LANES))

    def apply(e):
        def step(i, carry):
            rows = pl.ds(pl.multiple_of(i * 8, 8), 8)
            dest = pl.ds(pl.multiple_of(mine + i * 8, 8), 8)
            a = alpha[e]
            for j in range(lane_blocks):
                at = slice(j * LANES, (j + 1) * LANES)
                out[e, dest, at] = wv[e, rows, at] - a * own[e, rows, at]
            return carry

        lax.fori_loop(0, half // 8, step, 0)

    def next_send(n):
        if n >= 2 * total:
            return
        if n >= FLIGHT:
            before = n - FLIGHT
            if before < total:
                scatter(before).wait_send()
            else:
                gather(before - total).wait_send()
        if n < total:
            scatter(n).start()
        else:
            gather(n - total).start()

    for n in range(FLIGHT):
        next_send(n)
    for load in list(states) + [load for pair in loads for load in pair][1:]:
        load.start()
    after = {
        per - 1: [moments_out],
        per + 1: [columns_in],
        per + 5: [moments_in, normalise],
        per + 6: [tile_sums_in],
        per + 7: [plane_sums_in],
        per + 11: [scale_in, apply],
    }
    for n in range(2 * total):
        e, k = divmod(n, per)
        if n < total:
            if k == 0:
                loads[e][0].wait()
            scatter(n).wait_recv()
            next_send(n + FLIGHT)
            add_chunk(n)
        else:
            next_send(n + FLIGHT)
        for done in range(experts):
            for task in after.get(n - done * per, []):
                task(done)
    for n in range(2 * total - FLIGHT, 2 * total):
        gather(n - total).wait_send()
    for a in range(total):
        gather(a).wait_recv()


def write_out(sources, targets, sems):
    copies = []
    for source, target in zip(sources, targets):
        if source.ndim == 3:
            step = min(PIECE, source.shape[1])
            for e in range(source.shape[0]):
                for r in range(0, source.shape[1], step):
                    copies.append((source.at[e, pl.ds(r, step)], target.at[e, pl.ds(r, step)]))
        else:
            copies.append((source, target))
    copies = [pltpu.make_async_copy(a, b, sems.at[i]) for i, (a, b) in enumerate(copies)]
    for copy in copies:
        copy.start()
    for copy in copies:
        copy.wait()


def writer(a, b, c, x, y, z, sems):
    write_out((a, b, c), (x, y, z), sems)


def written(results):
    anywhere = pl.BlockSpec(memory_space=pl.ANY)
    hbm = pl.BlockSpec(memory_space=pltpu.HBM)
    big = results[0].shape
    count = big[0] * (big[1] // min(PIECE, big[1])) + 2
    return pl.pallas_call(
        writer,
        out_shape=tuple(jax.ShapeDtypeStruct(r.shape, r.dtype) for r in results),
        in_specs=[anywhere] * 3,
        out_specs=(hbm,) * 3,
        scratch_shapes=[pltpu.SemaphoreType.DMA((count,))],
        compiler_params=pltpu.CompilerParams(vmem_limit_bytes=1024 * 1024),
        name="write_out",
    )(*results)


def fused_body(n_row, n_col, grad_parts, weight, row_state, col_state):
    experts, half, cols = weight.shape
    blocks = half // LANES
    total = experts * (half // CHUNK)
    f32 = jnp.float32
    hbm = pl.BlockSpec(memory_space=pltpu.HBM)
    vmem = pl.BlockSpec(memory_space=pltpu.VMEM)
    dma = pltpu.SemaphoreType.DMA
    results = pl.pallas_call(
        functools.partial(kernel, n_row, n_col),
        out_shape=(
            pltpu.VMEM((experts, 2 * half, cols), f32),
            pltpu.VMEM(row_state.shape, f32),
            pltpu.VMEM(col_state.shape, f32),
        ),
        in_specs=[hbm] * 4,
        out_specs=(vmem, vmem, vmem),
        scratch_shapes=[
            pltpu.VMEM(row_state.shape, f32),
            pltpu.VMEM(col_state.shape, f32),
            pltpu.VMEM((experts, half, cols), f32),
            pltpu.VMEM((experts, half, cols), f32),
            pltpu.VMEM((experts, half, cols), f32),
            pltpu.VMEM((experts, half, LANES), f32),
            pltpu.VMEM((experts, 8, cols), f32),
            pltpu.VMEM((experts, 8, cols), f32),
            pltpu.VMEM((experts, 8, LANES), f32),
            pltpu.VMEM((experts, n_col, blocks, LANES), f32),
            pltpu.VMEM((experts, n_row, 1, cols), f32),
            pltpu.VMEM((experts, 2, 1, cols), f32),
            pltpu.VMEM((experts, n_col, 2, LANES), f32),
            pltpu.VMEM((experts, n_row, 3, LANES), f32),
            pltpu.VMEM((experts, 2, 3, LANES), f32),
            dma((2 * experts + 2,)),
            dma((FLIGHT,)),
            dma((total,)),
            dma((FLIGHT,)),
            dma((total,)),
            dma((experts, 2, n_col - 1)),
            dma((experts, 2, n_col - 1)),
            dma((experts, 2, n_row - 1)),
            dma((experts, 2, n_row - 1)),
            dma((experts, 2, 1)),
            dma((experts, 2, 1)),
        ],
        compiler_params=pltpu.CompilerParams(
            collective_id=0, has_side_effects=True, vmem_limit_bytes=30 * 1024 * 1024
        ),
        cost_estimate=pl.CostEstimate(
            flops=20 * weight.size, bytes_accessed=20 * weight.size, transcendentals=0
        ),
        name="fused_step",
    )(*[
        pltpu.with_memory_space_constraint(x, pltpu.HBM)
        for x in (grad_parts, weight, row_state, col_state)
    ])
    return written(results)


def solution(mesh):
    placed = (
        P("dp", None, "row", "col"),
        P(None, ("row", "dp"), "col"),
        P(None, ("row", "dp")),
        P(None, "col"),
    )
    body = fused_body if mesh.shape["dp"] == 2 else plain_body
    return jax.shard_map(
        functools.partial(body, mesh.shape["row"], mesh.shape["col"]),
        mesh=mesh,
        in_specs=placed,
        out_specs=(P(None, "row", "col"), P(None, ("row", "dp")), P(None, "col")),
        check_vma=False,
    )
```

```python
import functools

import jax
import jax.numpy as jnp
from jax import lax
from jax.experimental import pallas as pl
from jax.experimental.pallas import tpu as pltpu
from jax.sharding import PartitionSpec as P

DECAY = 1.0 - 2.0 ** (-0.8)
MESH = pl.DeviceIdType.MESH
LANES = 128
CHUNK = 32
FLIGHT = 4
PIECE = 128
TAIL = 4


def adafactor(grad, weight, row_state, col_state, reduce_rows, reduce_cols, reduce_all, width, height):
    sq = grad * grad + 1e-30
    row_local = jnp.sum(sq, axis=2)
    weight_local = jnp.sum(weight * weight, axis=(1, 2))
    row_total, weight_part = reduce_rows(row_local, weight_local)
    new_row = DECAY * row_state + (1.0 - DECAY) * row_total / width
    col_local = jnp.sum(sq, axis=1)
    moment_local = jnp.sum(new_row, axis=1)
    col_total, moment_total, weight_total = reduce_cols(col_local, moment_local, weight_part)
    new_col = DECAY * col_state + (1.0 - DECAY) * col_total / height
    row_mean = moment_total / height
    vhat = new_row[:, :, None] * new_col[:, None, :] / row_mean[:, None, None]
    update = grad / jnp.sqrt(vhat)
    update_total = reduce_all(jnp.sum(update * update, axis=(1, 2)))
    clip = jnp.maximum(1.0, jnp.sqrt(update_total / (height * width)))
    step_size = 0.3 * jnp.maximum(0.001, jnp.sqrt(weight_total / (height * width)))
    new_weight = weight - (step_size / clip)[:, None, None] * update
    return (new_weight, new_row, new_col)


def plain_body(n_row, n_col, grad_parts, weight, row_state, col_state):
    grad = lax.psum_scatter(grad_parts[0], "dp", scatter_dimension=1, tiled=True)

    def reduce_rows(row_local, weight_local):
        return (lax.psum(row_local, "col"), weight_local)

    def reduce_cols(col_local, moment_local, weight_part):
        col_total, moment_total = lax.psum((col_local, moment_local), ("dp", "row"))
        weight_total = lax.psum(weight_part, ("dp", "row", "col"))
        return (col_total, moment_total, weight_total)

    def reduce_all(value):
        return lax.psum(value, ("dp", "row", "col"))

    width = grad_parts.shape[3] * n_col
    height = grad_parts.shape[2] * n_row
    new_shard, new_row, new_col = adafactor(
        grad, weight, row_state, col_state, reduce_rows, reduce_cols, reduce_all, width, height
    )
    new_weight = lax.all_gather(new_shard, "dp", axis=1, tiled=True)
    return (new_weight, new_row, new_col)


def kernel(
    n_row, n_col, gp, w, rs_in, cs_in, out, nrow, ncol, tail,
    rs, cs, got, own, wv, part, colacc, colscale, alpha, rowbuf, colbuf, colpair, abuf, bbuf, bpair,
    load_sem, tail_sem, rs_send, rs_recv, ag_send, ag_recv,
    z_send, z_recv, y_send, y_recv, x_send, x_recv,
):
    experts, half, cols = w.shape
    width, height = cols * n_col, 2 * half * n_row
    blocks = half // LANES
    lane_blocks = cols // LANES
    per = half // CHUNK
    total = experts * per
    dp, row, col = lax.axis_index("dp"), lax.axis_index("row"), lax.axis_index("col")
    mine = pl.multiple_of(dp * half, CHUNK)
    theirs = pl.multiple_of((1 - dp) * half, CHUNK)
    partner = {"dp": 1 - dp}

    def col_peer(p):
        return {"col": lax.rem(col + p, n_col)}

    def row_peer(p):
        return {"row": lax.rem(row + p, n_row)}

    def dp_peer(p):
        return partner

    loads = []
    for e in range(experts):
        loads.append((
            pltpu.make_async_copy(gp.at[0, e, pl.ds(mine, half)], own.at[e], load_sem.at[2 * e]),
            pltpu.make_async_copy(w.at[e], wv.at[e], load_sem.at[2 * e + 1]),
        ))
    states = (
        pltpu.make_async_copy(rs_in, rs, load_sem.at[2 * experts]),
        pltpu.make_async_copy(cs_in, cs, load_sem.at[2 * experts + 1]),
    )
    loads[0][0].start()

    barrier = pltpu.get_barrier_semaphore()
    pl.semaphore_signal(barrier, inc=1, device_id=partner, device_id_type=MESH)
    for p in range(1, n_col):
        pl.semaphore_signal(barrier, inc=1, device_id=col_peer(p), device_id_type=MESH)
    for p in range(1, n_row):
        pl.semaphore_signal(barrier, inc=1, device_id=row_peer(p), device_id_type=MESH)
    pl.semaphore_wait(barrier, n_row + n_col - 1)

    def scatter(s):
        e, k = divmod(s, per)
        return pltpu.make_async_remote_copy(
            src_ref=gp.at[0, e, pl.ds(pl.multiple_of(theirs + k * CHUNK, CHUNK), CHUNK)],
            dst_ref=got.at[e, pl.ds(k * CHUNK, CHUNK)],
            send_sem=rs_send.at[s % FLIGHT], recv_sem=rs_recv.at[s],
            device_id=partner, device_id_type=MESH,
        )

    def gather(a):
        e, k = divmod(a, per)
        rows = out.at[e, pl.ds(pl.multiple_of(mine + k * CHUNK, CHUNK), CHUNK)]
        return pltpu.make_async_remote_copy(
            src_ref=rows,
            dst_ref=rows,
            send_sem=ag_send.at[a % FLIGHT], recv_sem=ag_recv.at[a],
            device_id=partner, device_id_type=MESH,
        )

    def exchange(buf, e, slot, count, peer_of, send, recv, which):
        return [
            pltpu.make_async_remote_copy(
                src_ref=buf.at[e, slot], dst_ref=buf.at[e, slot],
                send_sem=send.at[e, which, p - 1], recv_sem=recv.at[e, which, p - 1],
                device_id=peer_of(p), device_id_type=MESH,
            )
            for p in range(1, count)
        ]

    def row_exchange(e):
        return exchange(rowbuf, e, col, n_col, col_peer, z_send, z_recv, 0)

    def col_exchange(e):
        return exchange(colbuf, e, row, n_row, row_peer, y_send, y_recv, 0)

    def col_pair(e):
        return exchange(colpair, e, dp, 2, dp_peer, x_send, x_recv, 0)

    def a_exchange(e):
        return exchange(abuf, e, col, n_col, col_peer, z_send, z_recv, 1)

    def b_exchange(e):
        return exchange(bbuf, e, row, n_row, row_peer, y_send, y_recv, 1)

    def b_pair(e):
        return exchange(bpair, e, dp, 2, dp_peer, x_send, x_recv, 1)

    def start_all(copies):
        for copy in copies:
            copy.start()

    def wait_all(copies):
        for copy in copies:
            copy.wait()

    def summed(buf, e, count):
        value = buf[e, 0]
        for i in range(1, count):
            value = value + buf[e, i]
        return value

    def add_chunk(s):
        e, k = divmod(s, per)

        def step(i, acc):
            rows = pl.ds(pl.multiple_of(k * CHUNK + i * 8, 8), 8)
            g = own[e, rows, :] + got[e, rows, :]
            own[e, rows, :] = g
            sq = g * g + 1e-30
            lanes = sq[:, :LANES]
            for j in range(1, lane_blocks):
                lanes = lanes + sq[:, j * LANES:(j + 1) * LANES]
            part[e, rows, :] = lanes
            return acc + sq

        first = jnp.zeros((8, cols), jnp.float32) if k == 0 else colacc[e]
        colacc[e] = lax.fori_loop(0, CHUNK // 8, step, first)

    def moments_out(e):
        colbuf[e, row] = jnp.sum(colacc[e], axis=0, keepdims=True)
        for b in range(blocks):
            block = part[e, b * LANES:(b + 1) * LANES, :]
            rowbuf[e, col, b:b + 1, :] = jnp.sum(block.T, axis=0, keepdims=True)
        start_all(row_exchange(e))
        start_all(col_exchange(e))

    def columns_in(e):
        wait_all(col_exchange(e))
        colpair[e, dp] = summed(colbuf, e, n_row)
        start_all(col_pair(e))

    def moments_in(e):
        if e == 0:
            for load in states:
                load.wait()
        wait_all(row_exchange(e))
        row_total = summed(rowbuf, e, n_col)
        moment = jnp.zeros((1, LANES), jnp.float32)
        for b in range(blocks):
            at = slice(b * LANES, (b + 1) * LANES)
            new_row = DECAY * rs[e:e + 1, at] + (1.0 - DECAY) * row_total[b:b + 1, :] / width
            nrow[e:e + 1, at] = new_row
            moment = moment + new_row
            part[e, at, :] = jnp.broadcast_to(lax.rsqrt(new_row), (LANES, LANES)).T
        wait_all(col_pair(e))
        new_col = DECAY * cs[e:e + 1, :] + (1.0 - DECAY) * summed(colpair, e, 2) / height
        ncol[e:e + 1, :] = new_col
        colscale[e] = jnp.broadcast_to(lax.rsqrt(new_col), (8, cols))
        bbuf[e, row, 2:3, :] = moment

    def normalise(e):
        loads[e][1].wait()

        def step(i, sums):
            upd, wgt = sums
            rows = pl.ds(pl.multiple_of(i * 8, 8), 8)
            scale = part[e, rows, :]
            for j in range(lane_blocks):
                at = slice(j * LANES, (j + 1) * LANES)
                t = own[e, rows, at] * (scale * colscale[e, :, at])
                own[e, rows, at] = t
                upd = upd + t * t
                v = wv[e, rows, at]
                wgt = wgt + v * v
            return upd, wgt

        zero = jnp.zeros((8, LANES), jnp.float32)
        upd, wgt = lax.fori_loop(0, half // 8, step, (zero, zero))
        abuf[e, col, 0:1, :] = jnp.sum(upd, axis=0, keepdims=True)
        abuf[e, col, 1:2, :] = jnp.sum(wgt, axis=0, keepdims=True)
        start_all(a_exchange(e))

    def tile_sums_in(e):
        wait_all(a_exchange(e))
        bbuf[e, row, 0:2, :] = summed(abuf, e, n_col)
        start_all(b_exchange(e))

    def plane_sums_in(e):
        wait_all(b_exchange(e))
        bpair[e, dp] = summed(bbuf, e, n_row)
        start_all(b_pair(e))

    def scale_in(e):
        wait_all(b_pair(e))
        sums = jnp.sum(summed(bpair, e, 2), axis=1, keepdims=True)

        def whole(at):
            return sums[at:at + 1, :]

        size = float(width * height)
        row_mean = whole(2) / height
        clip = jnp.maximum(1.0, jnp.sqrt(row_mean * whole(0) / size))
        step_size = 0.3 * jnp.maximum(0.001, jnp.sqrt(whole(1) / size))
        alpha[e] = jnp.broadcast_to(step_size / clip * jnp.sqrt(row_mean), (8, LANES))

    def apply(e):
        def step(i, carry):
            rows = pl.ds(pl.multiple_of(i * 8, 8), 8)
            dest = pl.ds(pl.multiple_of(mine + i * 8, 8), 8)
            a = alpha[e]
            for j in range(lane_blocks):
                at = slice(j * LANES, (j + 1) * LANES)
                out[e, dest, at] = wv[e, rows, at] - a * own[e, rows, at]
            return carry

        lax.fori_loop(0, half // 8, step, 0)
        if e == experts - 1:
            tail_copy().start()

    def tail_copy():
        rows = pl.ds(pl.multiple_of(mine + half - TAIL * CHUNK, CHUNK), TAIL * CHUNK)
        return pltpu.make_async_copy(out.at[experts - 1, rows], tail, tail_sem)

    def next_send(n):
        if n >= 2 * total - TAIL:
            return
        if n >= FLIGHT:
            before = n - FLIGHT
            if before < total:
                scatter(before).wait_send()
            else:
                gather(before - total).wait_send()
        if n < total:
            scatter(n).start()
        else:
            gather(n - total).start()

    for n in range(FLIGHT):
        next_send(n)
    for load in list(states) + [load for pair in loads for load in pair][1:]:
        load.start()
    after = {
        per - 1: [moments_out],
        per + 1: [columns_in],
        per + 5: [moments_in, normalise],
        per + 6: [tile_sums_in],
        per + 7: [plane_sums_in],
        per + 11: [scale_in, apply],
    }
    for n in range(2 * total):
        e, k = divmod(n, per)
        if n < total:
            if k == 0:
                loads[e][0].wait()
            scatter(n).wait_recv()
            next_send(n + FLIGHT)
            add_chunk(n)
        else:
            next_send(n + FLIGHT)
        for done in range(experts):
            for task in after.get(n - done * per, []):
                task(done)
    tail_copy().wait()
    for n in range(2 * total - TAIL - FLIGHT, 2 * total - TAIL):
        gather(n - total).wait_send()
    for a in range(total - TAIL):
        gather(a).wait_recv()


def write_out(sources, targets, sems):
    copies = []
    for source, target in zip(sources, targets):
        if source.ndim == 3:
            step = min(PIECE, source.shape[1])
            for e in range(source.shape[0]):
                for r in range(0, source.shape[1], step):
                    copies.append((source.at[e, pl.ds(r, step)], target.at[e, pl.ds(r, step)]))
        else:
            copies.append((source, target))
    copies = [pltpu.make_async_copy(a, b, sems.at[i]) for i, (a, b) in enumerate(copies)]
    for copy in copies:
        copy.start()
    for copy in copies:
        copy.wait()


def writer(a, b, c, x, y, z, sems):
    write_out((a, b, c), (x, y, z), sems)


def written(results):
    anywhere = pl.BlockSpec(memory_space=pl.ANY)
    hbm = pl.BlockSpec(memory_space=pltpu.HBM)
    big = results[0].shape
    count = big[0] * (big[1] // min(PIECE, big[1])) + 2
    return pl.pallas_call(
        writer,
        out_shape=tuple(jax.ShapeDtypeStruct(r.shape, r.dtype) for r in results),
        in_specs=[anywhere] * 3,
        out_specs=(hbm,) * 3,
        scratch_shapes=[pltpu.SemaphoreType.DMA((count,))],
        compiler_params=pltpu.CompilerParams(vmem_limit_bytes=1024 * 1024),
        cost_estimate=pl.CostEstimate(
            flops=0, bytes_accessed=8 * results[0].size, transcendentals=0
        ),
        name="write_out",
    )(*results)


def fused_body(n_row, n_col, grad_parts, weight, row_state, col_state):
    experts, half, cols = weight.shape
    blocks = half // LANES
    total = experts * (half // CHUNK)
    f32 = jnp.float32
    hbm = pl.BlockSpec(memory_space=pltpu.HBM)
    vmem = pl.BlockSpec(memory_space=pltpu.VMEM)
    dma = pltpu.SemaphoreType.DMA
    results = pl.pallas_call(
        functools.partial(kernel, n_row, n_col),
        out_shape=(
            pltpu.VMEM((experts, 2 * half, cols), f32),
            pltpu.VMEM(row_state.shape, f32),
            pltpu.VMEM(col_state.shape, f32),
            pltpu.HBM((TAIL * CHUNK, cols), f32),
        ),
        in_specs=[hbm] * 4,
        out_specs=(vmem, vmem, vmem, hbm),
        scratch_shapes=[
            pltpu.VMEM(row_state.shape, f32),
            pltpu.VMEM(col_state.shape, f32),
            pltpu.VMEM((experts, half, cols), f32),
            pltpu.VMEM((experts, half, cols), f32),
            pltpu.VMEM((experts, half, cols), f32),
            pltpu.VMEM((experts, half, LANES), f32),
            pltpu.VMEM((experts, 8, cols), f32),
            pltpu.VMEM((experts, 8, cols), f32),
            pltpu.VMEM((experts, 8, LANES), f32),
            pltpu.VMEM((experts, n_col, blocks, LANES), f32),
            pltpu.VMEM((experts, n_row, 1, cols), f32),
            pltpu.VMEM((experts, 2, 1, cols), f32),
            pltpu.VMEM((experts, n_col, 2, LANES), f32),
            pltpu.VMEM((experts, n_row, 3, LANES), f32),
            pltpu.VMEM((experts, 2, 3, LANES), f32),
            dma((2 * experts + 2,)),
            dma,
            dma((FLIGHT,)),
            dma((total,)),
            dma((FLIGHT,)),
            dma((total,)),
            dma((experts, 2, n_col - 1)),
            dma((experts, 2, n_col - 1)),
            dma((experts, 2, n_row - 1)),
            dma((experts, 2, n_row - 1)),
            dma((experts, 2, 1)),
            dma((experts, 2, 1)),
        ],
        compiler_params=pltpu.CompilerParams(
            collective_id=0, has_side_effects=True, vmem_limit_bytes=30 * 1024 * 1024
        ),
        cost_estimate=pl.CostEstimate(
            flops=20 * weight.size, bytes_accessed=20 * weight.size, transcendentals=0
        ),
        name="fused_step",
    )(*[
        pltpu.with_memory_space_constraint(x, pltpu.HBM)
        for x in (grad_parts, weight, row_state, col_state)
    ])
    arriving = lax.ppermute(results[3], "dp", [(0, 1), (1, 0)])
    new_weight, new_row, new_col = written(results[:3])
    start = (1 - lax.axis_index("dp")) * half + half - TAIL * CHUNK
    new_weight = lax.dynamic_update_slice(new_weight, arriving[None], (experts - 1, start, 0))
    return (new_weight, new_row, new_col)


def solution(mesh):
    placed = (
        P("dp", None, "row", "col"),
        P(None, ("row", "dp"), "col"),
        P(None, ("row", "dp")),
        P(None, "col"),
    )
    body = fused_body if mesh.shape["dp"] == 2 else plain_body
    return jax.shard_map(
        functools.partial(body, mesh.shape["row"], mesh.shape["col"]),
        mesh=mesh,
        in_specs=placed,
        out_specs=(P(None, "row", "col"), P(None, ("row", "dp")), P(None, "col")),
        check_vma=False,
    )
```

```python
import functools

import jax
import jax.numpy as jnp
from jax import lax
from jax.experimental import pallas as pl
from jax.experimental.pallas import tpu as pltpu
from jax.sharding import PartitionSpec as P

DECAY = 1.0 - 2.0 ** (-0.8)
MESH = pl.DeviceIdType.MESH
LANES = 128
CHUNK = 32
FLIGHT = 4
PIECE = 128
TAIL = 4


def adafactor(grad, weight, row_state, col_state, reduce_rows, reduce_cols, reduce_all, width, height):
    sq = grad * grad + 1e-30
    row_local = jnp.sum(sq, axis=2)
    weight_local = jnp.sum(weight * weight, axis=(1, 2))
    row_total, weight_part = reduce_rows(row_local, weight_local)
    new_row = DECAY * row_state + (1.0 - DECAY) * row_total / width
    col_local = jnp.sum(sq, axis=1)
    moment_local = jnp.sum(new_row, axis=1)
    col_total, moment_total, weight_total = reduce_cols(col_local, moment_local, weight_part)
    new_col = DECAY * col_state + (1.0 - DECAY) * col_total / height
    row_mean = moment_total / height
    vhat = new_row[:, :, None] * new_col[:, None, :] / row_mean[:, None, None]
    update = grad / jnp.sqrt(vhat)
    update_total = reduce_all(jnp.sum(update * update, axis=(1, 2)))
    clip = jnp.maximum(1.0, jnp.sqrt(update_total / (height * width)))
    step_size = 0.3 * jnp.maximum(0.001, jnp.sqrt(weight_total / (height * width)))
    new_weight = weight - (step_size / clip)[:, None, None] * update
    return (new_weight, new_row, new_col)


def plain_body(n_row, n_col, grad_parts, weight, row_state, col_state):
    grad = lax.psum_scatter(grad_parts[0], "dp", scatter_dimension=1, tiled=True)

    def reduce_rows(row_local, weight_local):
        return (lax.psum(row_local, "col"), weight_local)

    def reduce_cols(col_local, moment_local, weight_part):
        col_total, moment_total = lax.psum((col_local, moment_local), ("dp", "row"))
        weight_total = lax.psum(weight_part, ("dp", "row", "col"))
        return (col_total, moment_total, weight_total)

    def reduce_all(value):
        return lax.psum(value, ("dp", "row", "col"))

    width = grad_parts.shape[3] * n_col
    height = grad_parts.shape[2] * n_row
    new_shard, new_row, new_col = adafactor(
        grad, weight, row_state, col_state, reduce_rows, reduce_cols, reduce_all, width, height
    )
    new_weight = lax.all_gather(new_shard, "dp", axis=1, tiled=True)
    return (new_weight, new_row, new_col)


def kernel(
    n_row, n_col, gp, w, rs_in, cs_in, out, nrow, ncol, tail,
    rs, cs, got, own, wv, part, colacc, colscale, alpha, rowbuf, colbuf, colpair, abuf, bbuf, bpair,
    load_sem, store_sem, tail_sem, rs_send, rs_recv, ag_send, ag_recv,
    z_send, z_recv, y_send, y_recv, x_send, x_recv,
):
    experts, half, cols = w.shape
    width, height = cols * n_col, 2 * half * n_row
    blocks = half // LANES
    lane_blocks = cols // LANES
    per = half // CHUNK
    total = experts * per
    dp, row, col = lax.axis_index("dp"), lax.axis_index("row"), lax.axis_index("col")
    mine = pl.multiple_of(dp * half, CHUNK)
    theirs = pl.multiple_of((1 - dp) * half, CHUNK)
    partner = {"dp": 1 - dp}

    def col_peer(p):
        return {"col": lax.rem(col + p, n_col)}

    def row_peer(p):
        return {"row": lax.rem(row + p, n_row)}

    def dp_peer(p):
        return partner

    loads = []
    for e in range(experts):
        loads.append((
            pltpu.make_async_copy(gp.at[0, e, pl.ds(mine, half)], own.at[e], load_sem.at[2 * e]),
            pltpu.make_async_copy(w.at[e], wv.at[e], load_sem.at[2 * e + 1]),
        ))
    states = (
        pltpu.make_async_copy(rs_in, rs, load_sem.at[2 * experts]),
        pltpu.make_async_copy(cs_in, cs, load_sem.at[2 * experts + 1]),
    )
    loads[0][0].start()

    barrier = pltpu.get_barrier_semaphore()
    pl.semaphore_signal(barrier, inc=1, device_id=partner, device_id_type=MESH)
    for p in range(1, n_col):
        pl.semaphore_signal(barrier, inc=1, device_id=col_peer(p), device_id_type=MESH)
    for p in range(1, n_row):
        pl.semaphore_signal(barrier, inc=1, device_id=row_peer(p), device_id_type=MESH)
    pl.semaphore_wait(barrier, n_row + n_col - 1)

    def scatter(s):
        e, k = divmod(s, per)
        return pltpu.make_async_remote_copy(
            src_ref=gp.at[0, e, pl.ds(pl.multiple_of(theirs + k * CHUNK, CHUNK), CHUNK)],
            dst_ref=got.at[e, pl.ds(k * CHUNK, CHUNK)],
            send_sem=rs_send.at[s % FLIGHT], recv_sem=rs_recv.at[s],
            device_id=partner, device_id_type=MESH,
        )

    def gather(a):
        e, k = divmod(a, per)
        return pltpu.make_async_remote_copy(
            src_ref=wv.at[e, pl.ds(k * CHUNK, CHUNK)],
            dst_ref=out.at[e, pl.ds(pl.multiple_of(mine + k * CHUNK, CHUNK), CHUNK)],
            send_sem=ag_send.at[a % FLIGHT], recv_sem=ag_recv.at[a],
            device_id=partner, device_id_type=MESH,
        )

    def exchange(buf, e, slot, count, peer_of, send, recv, which):
        return [
            pltpu.make_async_remote_copy(
                src_ref=buf.at[e, slot], dst_ref=buf.at[e, slot],
                send_sem=send.at[e, which, p - 1], recv_sem=recv.at[e, which, p - 1],
                device_id=peer_of(p), device_id_type=MESH,
            )
            for p in range(1, count)
        ]

    def row_exchange(e):
        return exchange(rowbuf, e, col, n_col, col_peer, z_send, z_recv, 0)

    def col_exchange(e):
        return exchange(colbuf, e, row, n_row, row_peer, y_send, y_recv, 0)

    def col_pair(e):
        return exchange(colpair, e, dp, 2, dp_peer, x_send, x_recv, 0)

    def a_exchange(e):
        return exchange(abuf, e, col, n_col, col_peer, z_send, z_recv, 1)

    def b_exchange(e):
        return exchange(bbuf, e, row, n_row, row_peer, y_send, y_recv, 1)

    def b_pair(e):
        return exchange(bpair, e, dp, 2, dp_peer, x_send, x_recv, 1)

    def start_all(copies):
        for copy in copies:
            copy.start()

    def wait_all(copies):
        for copy in copies:
            copy.wait()

    def summed(buf, e, count):
        value = buf[e, 0]
        for i in range(1, count):
            value = value + buf[e, i]
        return value

    def add_chunk(s):
        e, k = divmod(s, per)

        def step(i, acc):
            rows = pl.ds(pl.multiple_of(k * CHUNK + i * 8, 8), 8)
            g = own[e, rows, :] + got[e, rows, :]
            own[e, rows, :] = g
            sq = g * g + 1e-30
            lanes = sq[:, :LANES]
            for j in range(1, lane_blocks):
                lanes = lanes + sq[:, j * LANES:(j + 1) * LANES]
            part[e, rows, :] = lanes
            return acc + sq

        first = jnp.zeros((8, cols), jnp.float32) if k == 0 else colacc[e]
        colacc[e] = lax.fori_loop(0, CHUNK // 8, step, first)

    def moments_out(e):
        colbuf[e, row] = jnp.sum(colacc[e], axis=0, keepdims=True)
        for b in range(blocks):
            block = part[e, b * LANES:(b + 1) * LANES, :]
            rowbuf[e, col, b:b + 1, :] = jnp.sum(block.T, axis=0, keepdims=True)
        start_all(row_exchange(e))
        start_all(col_exchange(e))

    def columns_in(e):
        wait_all(col_exchange(e))
        colpair[e, dp] = summed(colbuf, e, n_row)
        start_all(col_pair(e))

    def moments_in(e):
        if e == 0:
            for load in states:
                load.wait()
        wait_all(row_exchange(e))
        row_total = summed(rowbuf, e, n_col)
        moment = jnp.zeros((1, LANES), jnp.float32)
        for b in range(blocks):
            at = slice(b * LANES, (b + 1) * LANES)
            new_row = DECAY * rs[e:e + 1, at] + (1.0 - DECAY) * row_total[b:b + 1, :] / width
            nrow[e:e + 1, at] = new_row
            moment = moment + new_row
            part[e, at, :] = jnp.broadcast_to(lax.rsqrt(new_row), (LANES, LANES)).T
        wait_all(col_pair(e))
        new_col = DECAY * cs[e:e + 1, :] + (1.0 - DECAY) * summed(colpair, e, 2) / height
        ncol[e:e + 1, :] = new_col
        colscale[e] = jnp.broadcast_to(lax.rsqrt(new_col), (8, cols))
        bbuf[e, row, 2:3, :] = moment

    def normalise(e):
        loads[e][1].wait()

        def step(i, sums):
            upd, wgt = sums
            rows = pl.ds(pl.multiple_of(i * 8, 8), 8)
            scale = part[e, rows, :]
            for j in range(lane_blocks):
                at = slice(j * LANES, (j + 1) * LANES)
                t = own[e, rows, at] * (scale * colscale[e, :, at])
                own[e, rows, at] = t
                upd = upd + t * t
                v = wv[e, rows, at]
                wgt = wgt + v * v
            return upd, wgt

        zero = jnp.zeros((8, LANES), jnp.float32)
        upd, wgt = lax.fori_loop(0, half // 8, step, (zero, zero))
        abuf[e, col, 0:1, :] = jnp.sum(upd, axis=0, keepdims=True)
        abuf[e, col, 1:2, :] = jnp.sum(wgt, axis=0, keepdims=True)
        start_all(a_exchange(e))

    def tile_sums_in(e):
        wait_all(a_exchange(e))
        bbuf[e, row, 0:2, :] = summed(abuf, e, n_col)
        start_all(b_exchange(e))

    def plane_sums_in(e):
        wait_all(b_exchange(e))
        bpair[e, dp] = summed(bbuf, e, n_row)
        start_all(b_pair(e))

    def scale_in(e):
        wait_all(b_pair(e))
        sums = jnp.sum(summed(bpair, e, 2), axis=1, keepdims=True)

        def whole(at):
            return sums[at:at + 1, :]

        size = float(width * height)
        row_mean = whole(2) / height
        clip = jnp.maximum(1.0, jnp.sqrt(row_mean * whole(0) / size))
        step_size = 0.3 * jnp.maximum(0.001, jnp.sqrt(whole(1) / size))
        alpha[e] = jnp.broadcast_to(step_size / clip * jnp.sqrt(row_mean), (8, LANES))

    def apply(e):
        def step(i, carry):
            rows = pl.ds(pl.multiple_of(i * 8, 8), 8)
            a = alpha[e]
            for j in range(lane_blocks):
                at = slice(j * LANES, (j + 1) * LANES)
                wv[e, rows, at] = wv[e, rows, at] - a * own[e, rows, at]
            return carry

        lax.fori_loop(0, half // 8, step, 0)
        if e == experts - 1:
            tail_copy().start()
        keep(e).start()

    def tail_copy():
        rows = pl.ds(half - TAIL * CHUNK, TAIL * CHUNK)
        return pltpu.make_async_copy(wv.at[experts - 1, rows], tail, tail_sem)

    def keep(e):
        return pltpu.make_async_copy(wv.at[e], out.at[e, pl.ds(mine, half)], store_sem.at[e])

    def next_send(n):
        if n >= 2 * total - TAIL:
            return
        if n >= FLIGHT:
            before = n - FLIGHT
            if before < total:
                scatter(before).wait_send()
            else:
                gather(before - total).wait_send()
        if n < total:
            scatter(n).start()
        else:
            gather(n - total).start()

    for n in range(FLIGHT):
        next_send(n)
    for load in list(states) + [load for pair in loads for load in pair][1:]:
        load.start()
    after = {
        per - 1: [moments_out],
        per + 1: [columns_in],
        per + 5: [moments_in, normalise],
        per + 6: [tile_sums_in],
        per + 7: [plane_sums_in],
        per + 11: [scale_in, apply],
    }
    for n in range(2 * total):
        e, k = divmod(n, per)
        if n < total:
            if k == 0:
                loads[e][0].wait()
            scatter(n).wait_recv()
            next_send(n + FLIGHT)
            add_chunk(n)
        else:
            next_send(n + FLIGHT)
        for done in range(experts):
            for task in after.get(n - done * per, []):
                task(done)
    tail_copy().wait()
    for e in range(experts):
        keep(e).wait()
    for n in range(2 * total - TAIL - FLIGHT, 2 * total - TAIL):
        gather(n - total).wait_send()
    for a in range(total - TAIL):
        gather(a).wait_recv()


def write_out(sources, targets, sems):
    copies = []
    for source, target in zip(sources, targets):
        if source.ndim == 3:
            step = min(PIECE, source.shape[1])
            for e in range(source.shape[0]):
                for r in range(0, source.shape[1], step):
                    copies.append((source.at[e, pl.ds(r, step)], target.at[e, pl.ds(r, step)]))
        else:
            copies.append((source, target))
    copies = [pltpu.make_async_copy(a, b, sems.at[i]) for i, (a, b) in enumerate(copies)]
    for copy in copies:
        copy.start()
    for copy in copies:
        copy.wait()


def writer(a, b, c, x, y, z, sems):
    write_out((a, b, c), (x, y, z), sems)


def written(results):
    anywhere = pl.BlockSpec(memory_space=pl.ANY)
    hbm = pl.BlockSpec(memory_space=pltpu.HBM)
    big = results[0].shape
    count = big[0] * (big[1] // min(PIECE, big[1])) + 2
    return pl.pallas_call(
        writer,
        out_shape=tuple(jax.ShapeDtypeStruct(r.shape, r.dtype) for r in results),
        in_specs=[anywhere] * 3,
        out_specs=(hbm,) * 3,
        scratch_shapes=[pltpu.SemaphoreType.DMA((count,))],
        compiler_params=pltpu.CompilerParams(vmem_limit_bytes=1024 * 1024),
        cost_estimate=pl.CostEstimate(
            flops=0, bytes_accessed=8 * results[0].size, transcendentals=0
        ),
        name="write_out",
    )(pltpu.with_memory_space_constraint(results[0], pltpu.HBM), *results[1:])


def fused_body(n_row, n_col, grad_parts, weight, row_state, col_state):
    experts, half, cols = weight.shape
    blocks = half // LANES
    total = experts * (half // CHUNK)
    f32 = jnp.float32
    hbm = pl.BlockSpec(memory_space=pltpu.HBM)
    vmem = pl.BlockSpec(memory_space=pltpu.VMEM)
    dma = pltpu.SemaphoreType.DMA
    results = pl.pallas_call(
        functools.partial(kernel, n_row, n_col),
        out_shape=(
            pltpu.HBM((experts, 2 * half, cols), f32),
            pltpu.VMEM(row_state.shape, f32),
            pltpu.VMEM(col_state.shape, f32),
            pltpu.HBM((TAIL * CHUNK, cols), f32),
        ),
        in_specs=[hbm] * 4,
        out_specs=(hbm, vmem, vmem, hbm),
        scratch_shapes=[
            pltpu.VMEM(row_state.shape, f32),
            pltpu.VMEM(col_state.shape, f32),
            pltpu.VMEM((experts, half, cols), f32),
            pltpu.VMEM((experts, half, cols), f32),
            pltpu.VMEM((experts, half, cols), f32),
            pltpu.VMEM((experts, half, LANES), f32),
            pltpu.VMEM((experts, 8, cols), f32),
            pltpu.VMEM((experts, 8, cols), f32),
            pltpu.VMEM((experts, 8, LANES), f32),
            pltpu.VMEM((experts, n_col, blocks, LANES), f32),
            pltpu.VMEM((experts, n_row, 1, cols), f32),
            pltpu.VMEM((experts, 2, 1, cols), f32),
            pltpu.VMEM((experts, n_col, 2, LANES), f32),
            pltpu.VMEM((experts, n_row, 3, LANES), f32),
            pltpu.VMEM((experts, 2, 3, LANES), f32),
            dma((2 * experts + 2,)),
            dma((experts,)),
            dma,
            dma((FLIGHT,)),
            dma((total,)),
            dma((FLIGHT,)),
            dma((total,)),
            dma((experts, 2, n_col - 1)),
            dma((experts, 2, n_col - 1)),
            dma((experts, 2, n_row - 1)),
            dma((experts, 2, n_row - 1)),
            dma((experts, 2, 1)),
            dma((experts, 2, 1)),
        ],
        compiler_params=pltpu.CompilerParams(
            collective_id=0, has_side_effects=True, vmem_limit_bytes=30 * 1024 * 1024
        ),
        cost_estimate=pl.CostEstimate(
            flops=20 * weight.size, bytes_accessed=20 * weight.size, transcendentals=0
        ),
        name="fused_step",
    )(*[
        pltpu.with_memory_space_constraint(x, pltpu.HBM)
        for x in (grad_parts, weight, row_state, col_state)
    ])
    arriving = lax.ppermute(results[3], "dp", [(0, 1), (1, 0)])
    new_weight, new_row, new_col = written(results[:3])
    start = (1 - lax.axis_index("dp")) * half + half - TAIL * CHUNK
    new_weight = lax.dynamic_update_slice(new_weight, arriving[None], (experts - 1, start, 0))
    return (new_weight, new_row, new_col)


def solution(mesh):
    placed = (
        P("dp", None, "row", "col"),
        P(None, ("row", "dp"), "col"),
        P(None, ("row", "dp")),
        P(None, "col"),
    )
    body = fused_body if mesh.shape["dp"] == 2 else plain_body
    return jax.shard_map(
        functools.partial(body, mesh.shape["row"], mesh.shape["col"]),
        mesh=mesh,
        in_specs=placed,
        out_specs=(P(None, "row", "col"), P(None, ("row", "dp")), P(None, "col")),
        check_vma=False,
    )
```

```python
import functools

import jax
import jax.numpy as jnp
from jax import lax
from jax.experimental import pallas as pl
from jax.experimental.pallas import tpu as pltpu
from jax.sharding import PartitionSpec as P

DECAY = 1.0 - 2.0 ** (-0.8)
MESH = pl.DeviceIdType.MESH
LANES = 128
CHUNK = 32
FLIGHT = 4
PIECE = 128
TAIL = 4


def adafactor(grad, weight, row_state, col_state, reduce_rows, reduce_cols, reduce_all, width, height):
    sq = grad * grad + 1e-30
    row_local = jnp.sum(sq, axis=2)
    weight_local = jnp.sum(weight * weight, axis=(1, 2))
    row_total, weight_part = reduce_rows(row_local, weight_local)
    new_row = DECAY * row_state + (1.0 - DECAY) * row_total / width
    col_local = jnp.sum(sq, axis=1)
    moment_local = jnp.sum(new_row, axis=1)
    col_total, moment_total, weight_total = reduce_cols(col_local, moment_local, weight_part)
    new_col = DECAY * col_state + (1.0 - DECAY) * col_total / height
    row_mean = moment_total / height
    vhat = new_row[:, :, None] * new_col[:, None, :] / row_mean[:, None, None]
    update = grad / jnp.sqrt(vhat)
    update_total = reduce_all(jnp.sum(update * update, axis=(1, 2)))
    clip = jnp.maximum(1.0, jnp.sqrt(update_total / (height * width)))
    step_size = 0.3 * jnp.maximum(0.001, jnp.sqrt(weight_total / (height * width)))
    new_weight = weight - (step_size / clip)[:, None, None] * update
    return (new_weight, new_row, new_col)


def plain_body(n_row, n_col, grad_parts, weight, row_state, col_state):
    grad = lax.psum_scatter(grad_parts[0], "dp", scatter_dimension=1, tiled=True)

    def reduce_rows(row_local, weight_local):
        return (lax.psum(row_local, "col"), weight_local)

    def reduce_cols(col_local, moment_local, weight_part):
        col_total, moment_total = lax.psum((col_local, moment_local), ("dp", "row"))
        weight_total = lax.psum(weight_part, ("dp", "row", "col"))
        return (col_total, moment_total, weight_total)

    def reduce_all(value):
        return lax.psum(value, ("dp", "row", "col"))

    width = grad_parts.shape[3] * n_col
    height = grad_parts.shape[2] * n_row
    new_shard, new_row, new_col = adafactor(
        grad, weight, row_state, col_state, reduce_rows, reduce_cols, reduce_all, width, height
    )
    new_weight = lax.all_gather(new_shard, "dp", axis=1, tiled=True)
    return (new_weight, new_row, new_col)


def kernel(
    n_row, n_col, gp, w, rs_in, cs_in, out, nrow, ncol, tail,
    rs, cs, got, own, wv, part, colacc, colscale, alpha, rowbuf, colbuf, colpair, abuf, bbuf, bpair,
    load_sem, store_sem, tail_sem, rs_send, rs_recv, ag_send, ag_recv,
    z_send, z_recv, y_send, y_recv, x_send, x_recv,
):
    experts, half, cols = w.shape
    width, height = cols * n_col, 2 * half * n_row
    blocks = half // LANES
    lane_blocks = cols // LANES
    per = half // CHUNK
    total = experts * per
    dp, row, col = lax.axis_index("dp"), lax.axis_index("row"), lax.axis_index("col")
    mine = pl.multiple_of(dp * half, CHUNK)
    theirs = pl.multiple_of((1 - dp) * half, CHUNK)
    partner = {"dp": 1 - dp}

    def col_peer(p):
        return {"col": lax.rem(col + p, n_col)}

    def row_peer(p):
        return {"row": lax.rem(row + p, n_row)}

    def dp_peer(p):
        return partner

    loads = []
    for e in range(experts):
        loads.append((
            pltpu.make_async_copy(gp.at[0, e, pl.ds(mine, half)], own.at[e], load_sem.at[2 * e]),
            pltpu.make_async_copy(w.at[e], wv.at[e], load_sem.at[2 * e + 1]),
        ))
    states = (
        pltpu.make_async_copy(rs_in, rs, load_sem.at[2 * experts]),
        pltpu.make_async_copy(cs_in, cs, load_sem.at[2 * experts + 1]),
    )
    loads[0][0].start()

    barrier = pltpu.get_barrier_semaphore()
    pl.semaphore_signal(barrier, inc=1, device_id=partner, device_id_type=MESH)
    for p in range(1, n_col):
        pl.semaphore_signal(barrier, inc=1, device_id=col_peer(p), device_id_type=MESH)
    for p in range(1, n_row):
        pl.semaphore_signal(barrier, inc=1, device_id=row_peer(p), device_id_type=MESH)
    pl.semaphore_wait(barrier, n_row + n_col - 1)

    def scatter(s):
        e, k = divmod(s, per)
        return pltpu.make_async_remote_copy(
            src_ref=gp.at[0, e, pl.ds(pl.multiple_of(theirs + k * CHUNK, CHUNK), CHUNK)],
            dst_ref=got.at[e, pl.ds(k * CHUNK, CHUNK)],
            send_sem=rs_send.at[s % FLIGHT], recv_sem=rs_recv.at[s],
            device_id=partner, device_id_type=MESH,
        )

    def gather(a):
        e, k = divmod(a, per)
        return pltpu.make_async_remote_copy(
            src_ref=wv.at[e, pl.ds(k * CHUNK, CHUNK)],
            dst_ref=out.at[e, pl.ds(pl.multiple_of(mine + k * CHUNK, CHUNK), CHUNK)],
            send_sem=ag_send.at[a % FLIGHT], recv_sem=ag_recv.at[a],
            device_id=partner, device_id_type=MESH,
        )

    def exchange(buf, e, slot, count, peer_of, send, recv, which):
        return [
            pltpu.make_async_remote_copy(
                src_ref=buf.at[e, slot], dst_ref=buf.at[e, slot],
                send_sem=send.at[e, which, p - 1], recv_sem=recv.at[e, which, p - 1],
                device_id=peer_of(p), device_id_type=MESH,
            )
            for p in range(1, count)
        ]

    def row_exchange(e):
        return exchange(rowbuf, e, col, n_col, col_peer, z_send, z_recv, 0)

    def col_exchange(e):
        return exchange(colbuf, e, row, n_row, row_peer, y_send, y_recv, 0)

    def col_pair(e):
        return exchange(colpair, e, dp, 2, dp_peer, x_send, x_recv, 0)

    def a_exchange(e):
        return exchange(abuf, e, col, n_col, col_peer, z_send, z_recv, 1)

    def b_exchange(e):
        return exchange(bbuf, e, row, n_row, row_peer, y_send, y_recv, 1)

    def b_pair(e):
        return exchange(bpair, e, dp, 2, dp_peer, x_send, x_recv, 1)

    def start_all(copies):
        for copy in copies:
            copy.start()

    def wait_all(copies):
        for copy in copies:
            copy.wait()

    def summed(buf, e, count):
        value = buf[e, 0]
        for i in range(1, count):
            value = value + buf[e, i]
        return value

    def add_chunk(s):
        e, k = divmod(s, per)

        def step(i, acc):
            rows = pl.ds(pl.multiple_of(k * CHUNK + i * 8, 8), 8)
            g = own[e, rows, :] + got[e, rows, :]
            own[e, rows, :] = g
            sq = g * g + 1e-30
            lanes = sq[:, :LANES]
            for j in range(1, lane_blocks):
                lanes = lanes + sq[:, j * LANES:(j + 1) * LANES]
            part[e, rows, :] = lanes
            return acc + sq

        first = jnp.zeros((8, cols), jnp.float32) if k == 0 else colacc[e]
        colacc[e] = lax.fori_loop(0, CHUNK // 8, step, first)

    def moments_out(e):
        colbuf[e, row] = jnp.sum(colacc[e], axis=0, keepdims=True)
        for b in range(blocks):
            block = part[e, b * LANES:(b + 1) * LANES, :]
            rowbuf[e, col, b:b + 1, :] = jnp.sum(block.T, axis=0, keepdims=True)
        start_all(row_exchange(e))
        start_all(col_exchange(e))

    def columns_in(e):
        wait_all(col_exchange(e))
        colpair[e, dp] = summed(colbuf, e, n_row)
        start_all(col_pair(e))

    def moments_in(e):
        if e == 0:
            for load in states:
                load.wait()
        wait_all(row_exchange(e))
        row_total = summed(rowbuf, e, n_col)
        moment = jnp.zeros((1, LANES), jnp.float32)
        for b in range(blocks):
            at = slice(b * LANES, (b + 1) * LANES)
            new_row = DECAY * rs[e:e + 1, at] + (1.0 - DECAY) * row_total[b:b + 1, :] / width
            nrow[e:e + 1, at] = new_row
            moment = moment + new_row
            part[e, at, :] = jnp.broadcast_to(lax.rsqrt(new_row), (LANES, LANES)).T
        wait_all(col_pair(e))
        new_col = DECAY * cs[e:e + 1, :] + (1.0 - DECAY) * summed(colpair, e, 2) / height
        ncol[e:e + 1, :] = new_col
        colscale[e] = jnp.broadcast_to(lax.rsqrt(new_col), (8, cols))
        bbuf[e, row, 2:3, :] = moment

    def normalise(e):
        loads[e][1].wait()

        def step(i, sums):
            upd, wgt = sums
            rows = pl.ds(pl.multiple_of(i * 8, 8), 8)
            scale = part[e, rows, :]
            for j in range(lane_blocks):
                at = slice(j * LANES, (j + 1) * LANES)
                t = own[e, rows, at] * (scale * colscale[e, :, at])
                own[e, rows, at] = t
                upd = upd + t * t
                v = wv[e, rows, at]
                wgt = wgt + v * v
            return upd, wgt

        zero = jnp.zeros((8, LANES), jnp.float32)
        upd, wgt = lax.fori_loop(0, half // 8, step, (zero, zero))
        abuf[e, col, 0:1, :] = jnp.sum(upd, axis=0, keepdims=True)
        abuf[e, col, 1:2, :] = jnp.sum(wgt, axis=0, keepdims=True)
        start_all(a_exchange(e))

    def tile_sums_in(e):
        wait_all(a_exchange(e))
        bbuf[e, row, 0:2, :] = summed(abuf, e, n_col)
        start_all(b_exchange(e))

    def plane_sums_in(e):
        wait_all(b_exchange(e))
        bpair[e, dp] = summed(bbuf, e, n_row)
        start_all(b_pair(e))

    def scale_in(e):
        wait_all(b_pair(e))
        sums = jnp.sum(summed(bpair, e, 2), axis=1, keepdims=True)

        def whole(at):
            return sums[at:at + 1, :]

        size = float(width * height)
        row_mean = whole(2) / height
        clip = jnp.maximum(1.0, jnp.sqrt(row_mean * whole(0) / size))
        step_size = 0.3 * jnp.maximum(0.001, jnp.sqrt(whole(1) / size))
        alpha[e] = jnp.broadcast_to(step_size / clip * jnp.sqrt(row_mean), (8, LANES))

    def apply(e):
        def step(i, carry):
            rows = pl.ds(pl.multiple_of(i * 8, 8), 8)
            a = alpha[e]
            for j in range(lane_blocks):
                at = slice(j * LANES, (j + 1) * LANES)
                wv[e, rows, at] = wv[e, rows, at] - a * own[e, rows, at]
            return carry

        lax.fori_loop(0, half // 8, step, 0)
        if e == experts - 1:
            tail_copy().start()
        keep(e).start()

    def tail_copy():
        rows = pl.ds(half - TAIL * CHUNK, TAIL * CHUNK)
        return pltpu.make_async_copy(wv.at[experts - 1, rows], tail, tail_sem)

    def keep(e):
        return pltpu.make_async_copy(wv.at[e], out.at[e, pl.ds(mine, half)], store_sem.at[e])

    def next_send(n):
        if n >= 2 * total - TAIL:
            return
        if n >= FLIGHT:
            before = n - FLIGHT
            if before < total:
                scatter(before).wait_send()
            else:
                gather(before - total).wait_send()
        if n < total:
            scatter(n).start()
        else:
            gather(n - total).start()

    for n in range(FLIGHT):
        next_send(n)
    for load in list(states) + [load for pair in loads for load in pair][1:]:
        load.start()
    after = {
        per - 1: [moments_out],
        per + 1: [columns_in],
        per + 5: [moments_in, normalise],
        per + 6: [tile_sums_in],
        per + 7: [plane_sums_in],
        per + 11: [scale_in, apply],
    }
    for n in range(2 * total):
        e, k = divmod(n, per)
        if n < total:
            if k == 0:
                loads[e][0].wait()
            scatter(n).wait_recv()
            next_send(n + FLIGHT)
            add_chunk(n)
        else:
            next_send(n + FLIGHT)
        for done in range(experts):
            for task in after.get(n - done * per, []):
                task(done)
    tail_copy().wait()
    for e in range(experts):
        keep(e).wait()
    for n in range(2 * total - TAIL - FLIGHT, 2 * total - TAIL):
        gather(n - total).wait_send()
    for a in range(total - TAIL):
        gather(a).wait_recv()


def writer(a, b, c, x, y, z):
    x[...] = a[...]
    y[...] = b[...]
    z[...] = c[...]


def written(results):
    big, row, col = results
    experts, rows, cols = big.shape
    tile = pl.BlockSpec((1, PIECE, cols), lambda e, i: (e, i, 0))
    small = [pl.BlockSpec(r.shape, lambda e, i: (0, 0)) for r in (row, col)]
    return pl.pallas_call(
        writer,
        grid=(experts, rows // PIECE),
        out_shape=tuple(jax.ShapeDtypeStruct(r.shape, r.dtype) for r in results),
        in_specs=[tile] + small,
        out_specs=(tile, *small),
        compiler_params=pltpu.CompilerParams(vmem_limit_bytes=8 * 1024 * 1024),
        cost_estimate=pl.CostEstimate(
            flops=0, bytes_accessed=8 * big.size, transcendentals=0
        ),
        name="write_out",
    )(pltpu.with_memory_space_constraint(big, pltpu.HBM), row, col)


def fused_body(n_row, n_col, grad_parts, weight, row_state, col_state):
    experts, half, cols = weight.shape
    blocks = half // LANES
    total = experts * (half // CHUNK)
    f32 = jnp.float32
    hbm = pl.BlockSpec(memory_space=pltpu.HBM)
    vmem = pl.BlockSpec(memory_space=pltpu.VMEM)
    dma = pltpu.SemaphoreType.DMA
    results = pl.pallas_call(
        functools.partial(kernel, n_row, n_col),
        out_shape=(
            pltpu.HBM((experts, 2 * half, cols), f32),
            pltpu.VMEM(row_state.shape, f32),
            pltpu.VMEM(col_state.shape, f32),
            pltpu.HBM((TAIL * CHUNK, cols), f32),
        ),
        in_specs=[hbm] * 4,
        out_specs=(hbm, vmem, vmem, hbm),
        scratch_shapes=[
            pltpu.VMEM(row_state.shape, f32),
            pltpu.VMEM(col_state.shape, f32),
            pltpu.VMEM((experts, half, cols), f32),
            pltpu.VMEM((experts, half, cols), f32),
            pltpu.VMEM((experts, half, cols), f32),
            pltpu.VMEM((experts, half, LANES), f32),
            pltpu.VMEM((experts, 8, cols), f32),
            pltpu.VMEM((experts, 8, cols), f32),
            pltpu.VMEM((experts, 8, LANES), f32),
            pltpu.VMEM((experts, n_col, blocks, LANES), f32),
            pltpu.VMEM((experts, n_row, 1, cols), f32),
            pltpu.VMEM((experts, 2, 1, cols), f32),
            pltpu.VMEM((experts, n_col, 2, LANES), f32),
            pltpu.VMEM((experts, n_row, 3, LANES), f32),
            pltpu.VMEM((experts, 2, 3, LANES), f32),
            dma((2 * experts + 2,)),
            dma((experts,)),
            dma,
            dma((FLIGHT,)),
            dma((total,)),
            dma((FLIGHT,)),
            dma((total,)),
            dma((experts, 2, n_col - 1)),
            dma((experts, 2, n_col - 1)),
            dma((experts, 2, n_row - 1)),
            dma((experts, 2, n_row - 1)),
            dma((experts, 2, 1)),
            dma((experts, 2, 1)),
        ],
        compiler_params=pltpu.CompilerParams(
            collective_id=0, has_side_effects=True, vmem_limit_bytes=30 * 1024 * 1024
        ),
        cost_estimate=pl.CostEstimate(
            flops=20 * weight.size, bytes_accessed=20 * weight.size, transcendentals=0
        ),
        name="fused_step",
    )(*[
        pltpu.with_memory_space_constraint(x, pltpu.HBM)
        for x in (grad_parts, weight, row_state, col_state)
    ])
    arriving = lax.ppermute(results[3], "dp", [(0, 1), (1, 0)])
    new_weight, new_row, new_col = written(results[:3])
    start = (1 - lax.axis_index("dp")) * half + half - TAIL * CHUNK
    new_weight = lax.dynamic_update_slice(new_weight, arriving[None], (experts - 1, start, 0))
    return (new_weight, new_row, new_col)


def solution(mesh):
    placed = (
        P("dp", None, "row", "col"),
        P(None, ("row", "dp"), "col"),
        P(None, ("row", "dp")),
        P(None, "col"),
    )
    body = fused_body if mesh.shape["dp"] == 2 else plain_body
    return jax.shard_map(
        functools.partial(body, mesh.shape["row"], mesh.shape["col"]),
        mesh=mesh,
        in_specs=placed,
        out_specs=(P(None, "row", "col"), P(None, ("row", "dp")), P(None, "col")),
        check_vma=False,
    )
```

```python
import functools

import jax
import jax.numpy as jnp
from jax import lax
from jax.experimental import pallas as pl
from jax.experimental.pallas import tpu as pltpu
from jax.sharding import PartitionSpec as P

DECAY = 1.0 - 2.0 ** (-0.8)
MESH = pl.DeviceIdType.MESH
LANES = 128
CHUNK = 64
FLIGHT = 3
PIECE = 128
TAIL = 2


def adafactor(grad, weight, row_state, col_state, reduce_rows, reduce_cols, reduce_all, width, height):
    sq = grad * grad + 1e-30
    row_local = jnp.sum(sq, axis=2)
    weight_local = jnp.sum(weight * weight, axis=(1, 2))
    row_total, weight_part = reduce_rows(row_local, weight_local)
    new_row = DECAY * row_state + (1.0 - DECAY) * row_total / width
    col_local = jnp.sum(sq, axis=1)
    moment_local = jnp.sum(new_row, axis=1)
    col_total, moment_total, weight_total = reduce_cols(col_local, moment_local, weight_part)
    new_col = DECAY * col_state + (1.0 - DECAY) * col_total / height
    row_mean = moment_total / height
    vhat = new_row[:, :, None] * new_col[:, None, :] / row_mean[:, None, None]
    update = grad / jnp.sqrt(vhat)
    update_total = reduce_all(jnp.sum(update * update, axis=(1, 2)))
    clip = jnp.maximum(1.0, jnp.sqrt(update_total / (height * width)))
    step_size = 0.3 * jnp.maximum(0.001, jnp.sqrt(weight_total / (height * width)))
    new_weight = weight - (step_size / clip)[:, None, None] * update
    return (new_weight, new_row, new_col)


def plain_body(n_row, n_col, grad_parts, weight, row_state, col_state):
    grad = lax.psum_scatter(grad_parts[0], "dp", scatter_dimension=1, tiled=True)

    def reduce_rows(row_local, weight_local):
        return (lax.psum(row_local, "col"), weight_local)

    def reduce_cols(col_local, moment_local, weight_part):
        col_total, moment_total = lax.psum((col_local, moment_local), ("dp", "row"))
        weight_total = lax.psum(weight_part, ("dp", "row", "col"))
        return (col_total, moment_total, weight_total)

    def reduce_all(value):
        return lax.psum(value, ("dp", "row", "col"))

    width = grad_parts.shape[3] * n_col
    height = grad_parts.shape[2] * n_row
    new_shard, new_row, new_col = adafactor(
        grad, weight, row_state, col_state, reduce_rows, reduce_cols, reduce_all, width, height
    )
    new_weight = lax.all_gather(new_shard, "dp", axis=1, tiled=True)
    return (new_weight, new_row, new_col)


def kernel(
    n_row, n_col, gp, w, rs_in, cs_in, out, nrow, ncol, tail,
    rs, cs, got, own, wv, part, colacc, colscale, alpha, rowbuf, colbuf, colpair, abuf, bbuf, bpair,
    load_sem, store_sem, tail_sem, rs_send, rs_recv, ag_send, ag_recv,
    z_send, z_recv, y_send, y_recv, x_send, x_recv,
):
    experts, half, cols = w.shape
    width, height = cols * n_col, 2 * half * n_row
    blocks = half // LANES
    lane_blocks = cols // LANES
    per = half // CHUNK
    total = experts * per
    dp, row, col = lax.axis_index("dp"), lax.axis_index("row"), lax.axis_index("col")
    mine = pl.multiple_of(dp * half, CHUNK)
    theirs = pl.multiple_of((1 - dp) * half, CHUNK)
    partner = {"dp": 1 - dp}

    def col_peer(p):
        return {"col": lax.rem(col + p, n_col)}

    def row_peer(p):
        return {"row": lax.rem(row + p, n_row)}

    def dp_peer(p):
        return partner

    loads = []
    for e in range(experts):
        loads.append((
            pltpu.make_async_copy(gp.at[0, e, pl.ds(mine, half)], own.at[e], load_sem.at[2 * e]),
            pltpu.make_async_copy(w.at[e], wv.at[e], load_sem.at[2 * e + 1]),
        ))
    states = (
        pltpu.make_async_copy(rs_in, rs, load_sem.at[2 * experts]),
        pltpu.make_async_copy(cs_in, cs, load_sem.at[2 * experts + 1]),
    )
    loads[0][0].start()

    barrier = pltpu.get_barrier_semaphore()
    pl.semaphore_signal(barrier, inc=1, device_id=partner, device_id_type=MESH)
    for p in range(1, n_col):
        pl.semaphore_signal(barrier, inc=1, device_id=col_peer(p), device_id_type=MESH)
    for p in range(1, n_row):
        pl.semaphore_signal(barrier, inc=1, device_id=row_peer(p), device_id_type=MESH)
    pl.semaphore_wait(barrier, n_row + n_col - 1)

    def scatter(s):
        e, k = divmod(s, per)
        return pltpu.make_async_remote_copy(
            src_ref=gp.at[0, e, pl.ds(pl.multiple_of(theirs + k * CHUNK, CHUNK), CHUNK)],
            dst_ref=got.at[e, pl.ds(k * CHUNK, CHUNK)],
            send_sem=rs_send.at[s % FLIGHT], recv_sem=rs_recv.at[s],
            device_id=partner, device_id_type=MESH,
        )

    def gather(a):
        e, k = divmod(a, per)
        return pltpu.make_async_remote_copy(
            src_ref=wv.at[e, pl.ds(k * CHUNK, CHUNK)],
            dst_ref=out.at[e, pl.ds(pl.multiple_of(mine + k * CHUNK, CHUNK), CHUNK)],
            send_sem=ag_send.at[a % FLIGHT], recv_sem=ag_recv.at[a],
            device_id=partner, device_id_type=MESH,
        )

    def exchange(buf, e, slot, count, peer_of, send, recv, which):
        return [
            pltpu.make_async_remote_copy(
                src_ref=buf.at[e, slot], dst_ref=buf.at[e, slot],
                send_sem=send.at[e, which, p - 1], recv_sem=recv.at[e, which, p - 1],
                device_id=peer_of(p), device_id_type=MESH,
            )
            for p in range(1, count)
        ]

    def row_exchange(e):
        return exchange(rowbuf, e, col, n_col, col_peer, z_send, z_recv, 0)

    def col_exchange(e):
        return exchange(colbuf, e, row, n_row, row_peer, y_send, y_recv, 0)

    def col_pair(e):
        return exchange(colpair, e, dp, 2, dp_peer, x_send, x_recv, 0)

    def a_exchange(e):
        return exchange(abuf, e, col, n_col, col_peer, z_send, z_recv, 1)

    def b_exchange(e):
        return exchange(bbuf, e, row, n_row, row_peer, y_send, y_recv, 1)

    def b_pair(e):
        return exchange(bpair, e, dp, 2, dp_peer, x_send, x_recv, 1)

    def start_all(copies):
        for copy in copies:
            copy.start()

    def wait_all(copies):
        for copy in copies:
            copy.wait()

    def summed(buf, e, count):
        value = buf[e, 0]
        for i in range(1, count):
            value = value + buf[e, i]
        return value

    def add_chunk(s):
        e, k = divmod(s, per)

        def step(i, acc):
            rows = pl.ds(pl.multiple_of(k * CHUNK + i * 8, 8), 8)
            g = own[e, rows, :] + got[e, rows, :]
            own[e, rows, :] = g
            sq = g * g + 1e-30
            lanes = sq[:, :LANES]
            for j in range(1, lane_blocks):
                lanes = lanes + sq[:, j * LANES:(j + 1) * LANES]
            part[e, rows, :] = lanes
            return acc + sq

        first = jnp.zeros((8, cols), jnp.float32) if k == 0 else colacc[e]
        colacc[e] = lax.fori_loop(0, CHUNK // 8, step, first)

    def moments_out(e):
        colbuf[e, row] = jnp.sum(colacc[e], axis=0, keepdims=True)
        for b in range(blocks):
            block = part[e, b * LANES:(b + 1) * LANES, :]
            rowbuf[e, col, b:b + 1, :] = jnp.sum(block.T, axis=0, keepdims=True)
        start_all(row_exchange(e))
        start_all(col_exchange(e))

    def columns_in(e):
        wait_all(col_exchange(e))
        colpair[e, dp] = summed(colbuf, e, n_row)
        start_all(col_pair(e))

    def moments_in(e):
        if e == 0:
            for load in states:
                load.wait()
        wait_all(row_exchange(e))
        row_total = summed(rowbuf, e, n_col)
        moment = jnp.zeros((1, LANES), jnp.float32)
        for b in range(blocks):
            at = slice(b * LANES, (b + 1) * LANES)
            new_row = DECAY * rs[e:e + 1, at] + (1.0 - DECAY) * row_total[b:b + 1, :] / width
            nrow[e:e + 1, at] = new_row
            moment = moment + new_row
            part[e, at, :] = jnp.broadcast_to(lax.rsqrt(new_row), (LANES, LANES)).T
        wait_all(col_pair(e))
        new_col = DECAY * cs[e:e + 1, :] + (1.0 - DECAY) * summed(colpair, e, 2) / height
        ncol[e:e + 1, :] = new_col
        colscale[e] = jnp.broadcast_to(lax.rsqrt(new_col), (8, cols))
        bbuf[e, row, 2:3, :] = moment

    def normalise(e):
        loads[e][1].wait()

        def step(i, sums):
            upd, wgt = sums
            rows = pl.ds(pl.multiple_of(i * 8, 8), 8)
            scale = part[e, rows, :]
            for j in range(lane_blocks):
                at = slice(j * LANES, (j + 1) * LANES)
                t = own[e, rows, at] * (scale * colscale[e, :, at])
                own[e, rows, at] = t
                upd = upd + t * t
                v = wv[e, rows, at]
                wgt = wgt + v * v
            return upd, wgt

        zero = jnp.zeros((8, LANES), jnp.float32)
        upd, wgt = lax.fori_loop(0, half // 8, step, (zero, zero))
        abuf[e, col, 0:1, :] = jnp.sum(upd, axis=0, keepdims=True)
        abuf[e, col, 1:2, :] = jnp.sum(wgt, axis=0, keepdims=True)
        start_all(a_exchange(e))

    def tile_sums_in(e):
        wait_all(a_exchange(e))
        bbuf[e, row, 0:2, :] = summed(abuf, e, n_col)
        start_all(b_exchange(e))

    def plane_sums_in(e):
        wait_all(b_exchange(e))
        bpair[e, dp] = summed(bbuf, e, n_row)
        start_all(b_pair(e))

    def scale_in(e):
        wait_all(b_pair(e))
        sums = jnp.sum(summed(bpair, e, 2), axis=1, keepdims=True)

        def whole(at):
            return sums[at:at + 1, :]

        size = float(width * height)
        row_mean = whole(2) / height
        clip = jnp.maximum(1.0, jnp.sqrt(row_mean * whole(0) / size))
        step_size = 0.3 * jnp.maximum(0.001, jnp.sqrt(whole(1) / size))
        alpha[e] = jnp.broadcast_to(step_size / clip * jnp.sqrt(row_mean), (8, LANES))

    def apply(e):
        def step(i, carry):
            rows = pl.ds(pl.multiple_of(i * 8, 8), 8)
            a = alpha[e]
            for j in range(lane_blocks):
                at = slice(j * LANES, (j + 1) * LANES)
                wv[e, rows, at] = wv[e, rows, at] - a * own[e, rows, at]
            return carry

        lax.fori_loop(0, half // 8, step, 0)
        if e == experts - 1:
            tail_copy().start()
        keep(e).start()

    def tail_copy():
        rows = pl.ds(half - TAIL * CHUNK, TAIL * CHUNK)
        return pltpu.make_async_copy(wv.at[experts - 1, rows], tail, tail_sem)

    def keep(e):
        return pltpu.make_async_copy(wv.at[e], out.at[e, pl.ds(mine, half)], store_sem.at[e])

    def next_send(n):
        if n >= 2 * total - TAIL:
            return
        if n >= FLIGHT:
            before = n - FLIGHT
            if before < total:
                scatter(before).wait_send()
            else:
                gather(before - total).wait_send()
        if n < total:
            scatter(n).start()
        else:
            gather(n - total).start()

    for n in range(FLIGHT):
        next_send(n)
    for load in list(states) + [load for pair in loads for load in pair][1:]:
        load.start()
    after = {
        per - 1: [moments_out],
        per: [columns_in],
        per + 2: [moments_in, normalise],
        per + 3: [tile_sums_in, plane_sums_in],
        per + 4: [scale_in, apply],
    }
    for n in range(2 * total):
        e, k = divmod(n, per)
        if n < total:
            if k == 0:
                loads[e][0].wait()
            scatter(n).wait_recv()
            next_send(n + FLIGHT)
            add_chunk(n)
        else:
            next_send(n + FLIGHT)
        for done in range(experts):
            for task in after.get(n - done * per, []):
                task(done)
    tail_copy().wait()
    for e in range(experts):
        keep(e).wait()
    for n in range(2 * total - TAIL - FLIGHT, 2 * total - TAIL):
        gather(n - total).wait_send()
    for a in range(total - TAIL):
        gather(a).wait_recv()


def writer(a, b, c, x, y, z):
    x[...] = a[...]
    y[...] = b[...]
    z[...] = c[...]


def written(results):
    big, row, col = results
    experts, rows, cols = big.shape
    tile = pl.BlockSpec((1, PIECE, cols), lambda e, i: (e, i, 0))
    small = [pl.BlockSpec(r.shape, lambda e, i: (0, 0)) for r in (row, col)]
    return pl.pallas_call(
        writer,
        grid=(experts, rows // PIECE),
        out_shape=tuple(jax.ShapeDtypeStruct(r.shape, r.dtype) for r in results),
        in_specs=[tile] + small,
        out_specs=(tile, *small),
        compiler_params=pltpu.CompilerParams(vmem_limit_bytes=8 * 1024 * 1024),
        cost_estimate=pl.CostEstimate(
            flops=0, bytes_accessed=8 * big.size, transcendentals=0
        ),
        name="write_out",
    )(pltpu.with_memory_space_constraint(big, pltpu.HBM), row, col)


def fused_body(n_row, n_col, grad_parts, weight, row_state, col_state):
    experts, half, cols = weight.shape
    blocks = half // LANES
    total = experts * (half // CHUNK)
    f32 = jnp.float32
    hbm = pl.BlockSpec(memory_space=pltpu.HBM)
    vmem = pl.BlockSpec(memory_space=pltpu.VMEM)
    dma = pltpu.SemaphoreType.DMA
    results = pl.pallas_call(
        functools.partial(kernel, n_row, n_col),
        out_shape=(
            pltpu.HBM((experts, 2 * half, cols), f32),
            pltpu.VMEM(row_state.shape, f32),
            pltpu.VMEM(col_state.shape, f32),
            pltpu.HBM((TAIL * CHUNK, cols), f32),
        ),
        in_specs=[hbm] * 4,
        out_specs=(hbm, vmem, vmem, hbm),
        scratch_shapes=[
            pltpu.VMEM(row_state.shape, f32),
            pltpu.VMEM(col_state.shape, f32),
            pltpu.VMEM((experts, half, cols), f32),
            pltpu.VMEM((experts, half, cols), f32),
            pltpu.VMEM((experts, half, cols), f32),
            pltpu.VMEM((experts, half, LANES), f32),
            pltpu.VMEM((experts, 8, cols), f32),
            pltpu.VMEM((experts, 8, cols), f32),
            pltpu.VMEM((experts, 8, LANES), f32),
            pltpu.VMEM((experts, n_col, blocks, LANES), f32),
            pltpu.VMEM((experts, n_row, 1, cols), f32),
            pltpu.VMEM((experts, 2, 1, cols), f32),
            pltpu.VMEM((experts, n_col, 2, LANES), f32),
            pltpu.VMEM((experts, n_row, 3, LANES), f32),
            pltpu.VMEM((experts, 2, 3, LANES), f32),
            dma((2 * experts + 2,)),
            dma((experts,)),
            dma,
            dma((FLIGHT,)),
            dma((total,)),
            dma((FLIGHT,)),
            dma((total,)),
            dma((experts, 2, n_col - 1)),
            dma((experts, 2, n_col - 1)),
            dma((experts, 2, n_row - 1)),
            dma((experts, 2, n_row - 1)),
            dma((experts, 2, 1)),
            dma((experts, 2, 1)),
        ],
        compiler_params=pltpu.CompilerParams(
            collective_id=0, has_side_effects=True, vmem_limit_bytes=30 * 1024 * 1024
        ),
        cost_estimate=pl.CostEstimate(
            flops=20 * weight.size, bytes_accessed=20 * weight.size, transcendentals=0
        ),
        name="fused_step",
    )(*[
        pltpu.with_memory_space_constraint(x, pltpu.HBM)
        for x in (grad_parts, weight, row_state, col_state)
    ])
    arriving = lax.ppermute(results[3], "dp", [(0, 1), (1, 0)])
    new_weight, new_row, new_col = written(results[:3])
    start = (1 - lax.axis_index("dp")) * half + half - TAIL * CHUNK
    new_weight = lax.dynamic_update_slice(new_weight, arriving[None], (experts - 1, start, 0))
    return (new_weight, new_row, new_col)


def solution(mesh):
    placed = (
        P("dp", None, "row", "col"),
        P(None, ("row", "dp"), "col"),
        P(None, ("row", "dp")),
        P(None, "col"),
    )
    body = fused_body if mesh.shape["dp"] == 2 else plain_body
    return jax.shard_map(
        functools.partial(body, mesh.shape["row"], mesh.shape["col"]),
        mesh=mesh,
        in_specs=placed,
        out_specs=(P(None, "row", "col"), P(None, ("row", "dp")), P(None, "col")),
        check_vma=False,
    )
```
